256 devices in a mesh: gx: 16 (over z_hi, y, core), gy: 16 (over z_lo, x).
Axes of the slice: x: 4, y: 4, z: 8 (z_hi: 2, z_lo: 4; z = z_hi * 4 + z_lo), core: 2. Of those that a mesh axis runs over, the one named last changes fastest.
Arguments:
- positions: float32 [16, 16, 3, 8192], P('gx', 'gy'), may hold values from 0 to 3
- velocities: float32 [16, 16, 3, 8192], P('gx', 'gy'), may hold values from -5 to 5
- spins: float32 [16, 16, 3, 8192], P('gx', 'gy'), may hold values from -5 to 5
- radii: float32 [16, 16, 8192], P('gx', 'gy'), may hold values from 0.4 to 0.6
- counts: int32 [16, 16], P('gx', 'gy'), may hold values from 1024 to 8192
- exports: int32 [16, 16, 8, 32], P('gx', 'gy'), may hold values from 0 to 63
- partners: int32 [16, 16, 128], P('gx', 'gy'), may hold values from 0 to 319
- masks: int32 [16, 16, 128, 16, 128], P('gx', 'gy'), may hold values from 0 to 255
Outputs:
- new_positions: float32 [16, 16, 3, 8192], P('gx', 'gy')
- new_velocities: float32 [16, 16, 3, 8192], P('gx', 'gy')
- new_spins: float32 [16, 16, 3, 8192], P('gx', 'gy')
The draws below stay inside these ranges and needn't reach their ends.
Inputs may be any that keep to these rules, and one draw needn't show every extreme that they name: The first counts spheres of a column are live; the others take no part. `exports`: indices of owned tiles; a tile may appear more than once. `partners`: slots below 64 are owned tiles, the others ghost tiles. `masks`: each word holds 8 bits.
All inputs are finite; a program needn't handle non-finite values.
Results may differ from the reference program's by a relative error of at most 0.0003.
Values sent between devices are 32-bit elements; how exact they have to be, the bound alone decides.
No kernel may reach another device: no remote copies, remote signals or barrier semaphores. Data moves between devices by JAX's collectives and lax.ppermute only.
A program may use at most 64 MiB of HBM per device.

```python
import math
import jax
import jax.numpy as jnp
import numpy as np
from jax import lax

TILE = 128
TILES = 64
EXPORT = 32
PARTNERS = 2
STEPS = 2
SPHERES = 8192
PAIRS = 128
SLOTS = 320
N_GX = 16
N_GY = 16


def touch_ends(entries, rng, low, high):
    index_at = [jax.random.randint(jax.random.fold_in(rng, axis), (), 0, length) for axis, length in enumerate(entries.shape)]
    widest = entries.shape.index(max(entries.shape))
    next_to = index_at[:widest] + [(index_at[widest] + 1) % entries.shape[widest]] + index_at[widest + 1:]
    return entries.at[tuple(index_at)].set(low).at[tuple(next_to)].set(high)


def levels(own_key, dims, shards, least, largest):
    factor_of, own = 1.0, jax.random.fold_in(own_key, 6)
    for axis_at, blocks in shards:
        heights = jnp.exp(jax.random.uniform(jax.random.fold_in(own, axis_at), (blocks,), jnp.float32, least / len(shards), largest / len(shards)))
        factor_of = factor_of * jnp.repeat(heights, dims[axis_at] // blocks).reshape([-1 if axis == axis_at else 1 for axis in range(len(dims))])
    return factor_of


def centred(own_key, extent, deviation, bound, cuts=(), held_as=jnp.bfloat16):
    level = levels(own_key, extent, cuts, -0.22, 0.18) if cuts else 1.0
    drawn = jax.random.normal(own_key, extent, jnp.float32) * deviation * level
    return jnp.minimum(jnp.maximum(drawn, -bound), bound).astype(held_as)


def setup_inputs(seed: int = 0) -> dict:
    streams_of = jax.random.split(jax.random.key(seed), 9)
    return {
        "positions": jnp.clip(3.0 * jax.random.uniform(streams_of[0], (N_GX, N_GY, 3, SPHERES), jnp.float32) ** levels(streams_of[0], (N_GX, N_GY, 3, SPHERES), ((0, 16), (1, 16)), -0.2, 0.2), 0.0, 3.0),
        "velocities": centred(streams_of[1], (N_GX, N_GY, 3, SPHERES), 1.0, 5.0, ((0, 16), (1, 16)), jnp.float32),
        "spins": centred(streams_of[2], (N_GX, N_GY, 3, SPHERES), 1.0, 5.0, ((0, 16), (1, 16)), jnp.float32),
        "radii": jnp.clip(jnp.exp(math.log(0.6) - 0.40546513 * jax.random.uniform(streams_of[3], (N_GX, N_GY, SPHERES), jnp.float32) ** levels(streams_of[3], (N_GX, N_GY, SPHERES), ((0, 16), (1, 16)), -0.2, 0.2)), 0.4, 0.6),
        "counts": touch_ends(jax.random.randint(streams_of[4], (N_GX, N_GY), SPHERES // 8, SPHERES + 1), jax.random.fold_in(streams_of[4], 1), SPHERES // 8, SPHERES).astype(jnp.int32),
        "exports": touch_ends(jax.random.randint(streams_of[5], (N_GX, N_GY, 8, EXPORT), 0, TILES), jax.random.fold_in(streams_of[5], 1), 0, TILES - 1).astype(jnp.int32),
        "partners": touch_ends(jax.random.randint(streams_of[6], (N_GX, N_GY, PAIRS), 0, SLOTS), jax.random.fold_in(streams_of[6], 1), 0, SLOTS - 1).astype(jnp.int32),
        "masks": touch_ends(jax.random.randint(streams_of[7], (N_GX, N_GY, PAIRS, 16, TILE), 0, 256), jax.random.fold_in(streams_of[7], 1), 0, 255).astype(jnp.int32),
    }


stiffness = 1.0
damping_normal = 0.5
damping_tangent = 0.3
softening = 0.05
time_step = 0.25
column_width = 3.0
gravity = 1.0
mass_scale = 8.0
offsets = ((1, 0), (-1, 0), (0, 1), (0, -1), (1, 1), (1, -1), (-1, 1), (-1, -1))

def unpack_bits(words):
    shifts = jnp.arange(8, dtype=jnp.int32)
    bits = jnp.bitwise_and(jnp.right_shift(words[:, :, None, :], shifts[None, None, :, None]), 1)
    bits = bits.reshape(words.shape[0], words.shape[1] * 8, words.shape[2])
    return jnp.swapaxes(bits, 1, 2).astype(jnp.float32)

def cross(left, right):
    return (left[1] * right[2] - left[2] * right[1], left[2] * right[0] - left[0] * right[2], left[0] * right[1] - left[1] * right[0])

def block_forces(tiles, partner, words, first):
    number = partner.shape[0]
    slots = tiles.shape[1]
    owner = ((first + jnp.arange(number, dtype=jnp.int32)) // PARTNERS).astype(jnp.int32)
    left = jnp.take(tiles, owner, axis=1)[:, :, :, None]
    right = jnp.take(tiles, partner, axis=1)[:, :, None, :]
    weight = unpack_bits(words) * left[10] * right[10]
    separation = [right[k] - left[k] for k in range(3)]
    dist = jnp.sqrt(separation[0] * separation[0] + separation[1] * separation[1] + separation[2] * separation[2] + softening * softening)
    normal = [c / dist for c in separation]
    rad_i = left[9]
    rad_j = right[9]
    intersection = jnp.maximum(rad_i + rad_j - dist, 0.0)
    root = jnp.sqrt(rad_i * rad_j / (rad_i + rad_j) * intersection)
    spin_sum = [rad_i * left[6 + k] + rad_j * right[6 + k] for k in range(3)]
    turning = cross(spin_sum, normal)
    slip = [right[3 + k] - left[3 + k] - turning[k] for k in range(3)]
    speed_n = slip[0] * normal[0] + slip[1] * normal[1] + slip[2] * normal[2]
    push = weight * root * (stiffness * intersection - damping_normal * speed_n)
    drag = weight * root * damping_tangent
    force_j = [push * normal[k] - drag * (slip[k] - speed_n * normal[k]) for k in range(3)]
    twist = cross(normal, force_j)
    own_terms = jnp.stack([-lax.optimization_barrier(jnp.sum(f, axis=2)) for f in force_j] + [-lax.optimization_barrier(jnp.sum(rad_i * t, axis=2)) for t in twist], axis=1)
    other_terms = jnp.stack([lax.optimization_barrier(jnp.sum(f, axis=1)) for f in force_j] + [-lax.optimization_barrier(jnp.sum(rad_j * t, axis=1)) for t in twist], axis=1)
    places = jnp.arange(slots, dtype=jnp.int32)
    own_hot = (owner[:, None] == places[None, :]).astype(jnp.float32)
    other_hot = (partner[:, None] == places[None, :]).astype(jnp.float32)
    total = jnp.einsum('pt,pcs->cts', own_hot, own_terms, precision=lax.Precision.HIGHEST)
    return total + jnp.einsum('pt,pcs->cts', other_hot, other_terms, precision=lax.Precision.HIGHEST)

def contact_forces(tiles, partners, words, blocks):
    size = 4 * PARTNERS

    def one_block(index, total):
        first = (index * size).astype(jnp.int32)
        part = lax.dynamic_slice_in_dim(partners, first, size, 0)
        word = lax.dynamic_slice_in_dim(words, first, size, 0)
        return total + block_forces(tiles, part, word, first)
    start = jnp.zeros((6, tiles.shape[1], tiles.shape[2]), jnp.float32)
    return lax.fori_loop(0, blocks, one_block, start)

def advance(position, velocity, spin, radius, live, force):
    mass = mass_scale * radius * radius * radius
    inertia = 0.4 * mass * radius * radius
    lift = jnp.array([0.0, 0.0, -gravity], jnp.float32)[:, None, None]
    velocity = velocity + time_step * live * (force[..., 0:3, :, :] / mass + lift)
    spin = spin + time_step * live * force[..., 3:6, :, :] / inertia
    position = position + time_step * live * velocity
    return (position, velocity, spin)

def reference(positions, velocities, spins, radii, counts, exports, partners, masks):
    cols_x = positions.shape[0]
    cols_y = positions.shape[1]
    index = jnp.arange(TILES * TILE, dtype=jnp.int32)
    live = (index[None, None, :] < counts[:, :, None]).astype(jnp.float32)
    live = live.reshape(cols_x, cols_y, 1, TILES, TILE)
    radius = radii.reshape(cols_x, cols_y, 1, TILES, TILE)
    position = positions.reshape(cols_x, cols_y, 3, TILES, TILE)
    velocity = velocities.reshape(cols_x, cols_y, 3, TILES, TILE)
    spin = spins.reshape(cols_x, cols_y, 3, TILES, TILE)
    blocks = PAIRS // (4 * PARTNERS)
    places = jnp.arange(TILES, dtype=jnp.int32)

    def pick(state, chosen):
        taken = jnp.take(state, chosen.reshape(-1), axis=1)
        return taken.reshape(state.shape[0], 8, chosen.shape[1], TILE)
    for step in range(STEPS):
        state = jnp.concatenate([position, velocity, spin, radius, live], axis=2)
        sent = jax.vmap(jax.vmap(pick))(state, exports)
        pieces = [state]
        for which in range(8):
            step_x, step_y = offsets[which]
            block = jnp.roll(sent[:, :, :, which], (step_x, step_y), axis=(0, 1))
            moved = np.zeros((11, 1, 1), np.float32)
            moved[0] = -step_x * column_width
            moved[1] = -step_y * column_width
            pieces.append(block + jnp.asarray(moved))
        tiles = jnp.concatenate(pieces, axis=3)
        flat = tiles.reshape(cols_x * cols_y, 11, tiles.shape[3], TILE)
        flat_pairs = partners.reshape(cols_x * cols_y, PAIRS)
        flat_masks = masks.reshape(cols_x * cols_y, PAIRS, 16, TILE)
        force = lax.map(lambda item: contact_forces(item[0], item[1], item[2], blocks), (flat, flat_pairs, flat_masks))
        force = force.reshape(cols_x, cols_y, 6, tiles.shape[3], TILE)
        total = force[:, :, :, :TILES]
        for which in range(8):
            step_x, step_y = offsets[which]
            slot = force[:, :, :, TILES + which * EXPORT:TILES + (which + 1) * EXPORT]
            back = jnp.roll(slot, (-step_x, -step_y), axis=(0, 1))
            chooser = (exports[:, :, which, :, None] == places).astype(jnp.float32)
            total = total + jnp.einsum('xyet,xycea->xycta', chooser, back, precision=lax.Precision.HIGHEST)
        position, velocity, spin = advance(position, velocity, spin, radius, live, total)
    shape = (cols_x, cols_y, 3, TILES * TILE)
    return (position.reshape(shape), velocity.reshape(shape), spin.reshape(shape))
```

```python
import functools

import jax
import jax.numpy as jnp
from jax import lax
from jax.experimental import pallas as pl
from jax.experimental.pallas import tpu as pltpu
from jax.sharding import PartitionSpec as P

TILE = 128
STEPS = 2
BLOCK = 32

stiffness = 1.0
damping_normal = 0.5
damping_tangent = 0.3
softening = 0.05
time_step = 0.25
column_width = 3.0
gravity = 1.0
mass_scale = 8.0

DEAD = -10.0

VMEM = pl.BlockSpec(memory_space=pltpu.VMEM)
SMEM = pl.BlockSpec(memory_space=pltpu.SMEM)
VMEM_LIMIT = 48 * 1024 * 1024


def swap(value, axis, odd):
    count = lax.axis_size(axis)
    pairs = []
    for i in range(odd, count, 2):
        k = (i + 1) % count
        pairs += [(i, k), (k, i)]
    return lax.ppermute(value, axis, pairs)


def params():
    return pltpu.CompilerParams(vmem_limit_bytes=VMEM_LIMIT)


def cost(flops, size):
    return pl.CostEstimate(flops=flops, bytes_accessed=size, transcendentals=0)


def cross(a, b):
    return (
        a[1] * b[2] - a[2] * b[1],
        a[2] * b[0] - a[0] * b[2],
        a[0] * b[1] - a[1] * b[0],
    )


FIELDS = 11


def split(value):
    high = value.astype(jnp.bfloat16).astype(jnp.float32)
    rest = value - high
    middle = rest.astype(jnp.bfloat16).astype(jnp.float32)
    return high, middle, rest - middle


def fill_constants(spread, sums):
    sub = lax.broadcasted_iota(jnp.int32, (64, TILE), 0)
    for c in range(FIELDS):
        here = (lax.rem(sub, 16) == min(c, 9)) & (sub < 48)
        for ref in spread:
            ref[:, c * TILE : (c + 1) * TILE] = here.astype(jnp.float32).astype(jnp.bfloat16)
    row = lax.broadcasted_iota(jnp.int32, (16, 6 * TILE), 0)
    column = lax.broadcasted_iota(jnp.int32, (16, 6 * TILE), 1) // TILE
    sums[...] = (row == column).astype(jnp.float32).astype(jnp.bfloat16)


def combine(rec_i, rec_j, spread, both):
    high, middle, low = split(rec_i)
    sub = lax.broadcasted_iota(jnp.int32, (16, TILE), 0)
    for c in range(10):
        rows = jnp.where(
            sub == 0,
            high[c : c + 1],
            jnp.where(sub == 1, middle[c : c + 1], jnp.where(sub == 2, low[c : c + 1], 0.0)),
        )
        if c < 6:
            rows = -rows
        spread[48:64, c * TILE : (c + 1) * TILE] = rows.astype(jnp.bfloat16)
    high, middle, low = split(rec_j)
    left = jnp.concatenate(
        [high, middle, low, jnp.ones((16, TILE), jnp.float32), jnp.zeros((64, TILE), jnp.float32)], axis=0
    )
    left = jnp.transpose(left)[:, 0:64].astype(jnp.bfloat16)
    both[...] = jnp.dot(left, spread[...], preferred_element_type=jnp.float32)


def pair_forces(rec_i, rec_j, words, both, parts, sums):
    radius_i = rec_i[9:10, :]
    radius_j = rec_j[9:10, :]
    scaled = damping_tangent * radius_i
    sub = lax.broadcasted_iota(jnp.int32, (8, TILE), 0)
    bit = jnp.left_shift(1, sub)
    sums_i = [jnp.zeros((8, TILE), jnp.float32) for _ in range(6)]
    for first in range(0, TILE, BLOCK):
        field = [both[first : first + BLOCK, c * TILE : (c + 1) * TILE] for c in range(FIELDS)]
        r, dv, spin = field[0:3], field[3:6], field[6:9]
        d2 = r[0] * r[0] + r[1] * r[1] + (r[2] * r[2] + softening * softening)
        inv = lax.rsqrt(d2)
        inter = jnp.maximum(field[9] - d2 * inv, 0.0)
        top = field[10] * radius_i * inter
        root = field[10] * scaled * inter * lax.rsqrt(jnp.maximum(top * field[9], 1e-30))
        hit = jnp.concatenate(
            [
                (jnp.broadcast_to(words[w : w + 1, :], (8, TILE)) & bit) != 0
                for w in range(first // 8, (first + BLOCK) // 8)
            ],
            axis=0,
        )
        k2 = jnp.where(hit, root, 0.0)
        k3 = k2 * inv
        speed_n = (dv[0] * r[0] + dv[1] * r[1] + dv[2] * r[2]) * inv
        k1 = k3 * (
            (stiffness / damping_tangent) * inter
            - ((damping_normal - damping_tangent) / damping_tangent) * speed_n
        )
        turn = cross(spin, r)
        u = [dv[c] - inv * turn[c] for c in range(3)]
        terms = [k2 * u[c] - k1 * r[c] for c in range(3)] + [k3 * t for t in cross(r, u)]
        for c in range(6):
            part = terms[c]
            sums_i[c] = sums_i[c] + sum(part[8 * q : 8 * q + 8] for q in range(BLOCK // 8))
            high = part.astype(jnp.bfloat16)
            low = (part - high.astype(jnp.float32)).astype(jnp.bfloat16)
            parts[first : first + BLOCK, c * TILE : (c + 1) * TILE] = high
            parts[first : first + BLOCK, (6 + c) * TILE : (7 + c) * TILE] = low
    over = (((1,), (1,)), ((), ()))
    back = lax.dot_general(sums[...], parts[:, 0 : 6 * TILE], over, preferred_element_type=jnp.float32)
    back = back + lax.dot_general(
        sums[...], parts[:, 6 * TILE : 12 * TILE], over, preferred_element_type=jnp.float32
    )
    own = jnp.zeros((8, TILE), jnp.float32)
    for c in range(6):
        own = jnp.where(sub == c, jnp.sum(sums_i[c], axis=0, keepdims=True), own)
    own = own * jnp.where(sub < 3, 1.0, radius_i)
    back = back[0:8] * jnp.where(sub < 3, -1.0, radius_j)
    return own, back


def load_tiles(table, first, source, number):
    radius = source[9]
    for c in range(10):
        value = source[c] * radius if 6 <= c < 9 else source[c]
        table[pl.ds(first * 16 + c, number, stride=16), :] = value


def run_pairs(table, force, masks, partners, alive, low, high, scratch, part=(0, 1, 1)):
    chosen, spread_a, spread_b, both_a, both_b, parts_a, parts_b, sums = scratch
    fill_constants((spread_a, spread_b), sums)
    last = force.shape[0] - 1
    table[last * 16 : last * 16 + 16] = jnp.full((16, TILE), DEAD, jnp.float32)
    force[last] = jnp.zeros((8, TILE), jnp.float32)

    def place_of(slot):
        return slot if low == 0 else slot - (low - 64)

    def scan(p, found):
        slot = partners[p]
        good = (slot >= low) & (slot < high) & (alive[p // 2] > 0) & (alive[slot] > 0)
        chosen[found] = p
        return found + good.astype(jnp.int32)

    found = lax.fori_loop(0, 128, scan, 0)
    origin, number = found * part[0] // part[2], found * part[1] // part[2]

    def entry(n):
        n = jnp.minimum(n + origin, 127)
        p = jnp.where(n < number, chosen[n], 0)
        owner = jnp.where(n < number, p // 2, last)
        place = jnp.where(n < number, place_of(partners[p]), last)
        return p, owner, place

    def record(tile):
        return table[pl.ds(pl.multiple_of(tile * 16, 16), 16), :]

    def prepare(item, spread, both):
        combine(record(item[1]), record(item[2]), spread, both)

    def forces(item, both, parts):
        return pair_forces(record(item[1]), record(item[2]), masks[item[0]], both, parts, sums)

    def add(item, result):
        force[item[1]] = force[item[1]] + result[0]
        force[item[2]] = force[item[2]] + result[1]

    prepare(entry(0), spread_a, both_a)

    def two(t, carry):
        first, second, third = entry(2 * t), entry(2 * t + 1), entry(2 * t + 2)
        prepare(second, spread_b, both_b)
        one = forces(first, both_a, parts_a)
        prepare(third, spread_a, both_a)
        other = forces(second, both_b, parts_b)
        add(first, one)
        add(second, other)
        return carry

    lax.fori_loop(0, (number - origin + 1) // 2, two, 0)


def pair_scratch(tiles):
    return [
        pltpu.VMEM(((tiles + 1) * 16, TILE), jnp.float32),
        pltpu.VMEM((tiles + 1, 8, TILE), jnp.float32),
        pltpu.SMEM((129,), jnp.int32),
        pltpu.VMEM((64, FIELDS * TILE), jnp.bfloat16),
        pltpu.VMEM((64, FIELDS * TILE), jnp.bfloat16),
        pltpu.VMEM((TILE, FIELDS * TILE), jnp.float32),
        pltpu.VMEM((TILE, FIELDS * TILE), jnp.float32),
        pltpu.VMEM((TILE, 12 * TILE), jnp.bfloat16),
        pltpu.VMEM((TILE, 12 * TILE), jnp.bfloat16),
        pltpu.VMEM((16, 6 * TILE), jnp.bfloat16),
    ]


def own_kernel(part, partners, alive, state, masks, start, own_force, table, force, *scratch):
    table[...] = jnp.zeros_like(table)
    load_tiles(table, 0, state, 64)
    force[0:64] = start[...]
    run_pairs(table, force, masks, partners, alive, 0, 64, scratch, part)
    own_force[...] = force[0:64]


def face_kernel(partners, alive, state, masks, ghost, start, own_force, ghost_force, table, force, *scratch):
    table[...] = jnp.zeros_like(table)
    load_tiles(table, 0, state, 64)
    load_tiles(table, 64, ghost, 64)
    force[0:64] = start[...]
    force[64:128] = jnp.zeros((64, 8, TILE), jnp.float32)
    run_pairs(table, force, masks, partners, alive, 64, 128, scratch)
    own_force[...] = force[0:64]
    ghost_force[...] = force[64:128]


def far_kernel(
    partners, alive, state, masks, even, odd, start, own_force, even_force, odd_force, table, force, *scratch
):
    table[...] = jnp.zeros_like(table)
    load_tiles(table, 0, state, 64)
    load_tiles(table, 64, even, 96)
    load_tiles(table, 160, odd, 96)
    force[0:64] = start[...]
    force[64:256] = jnp.zeros((192, 8, TILE), jnp.float32)
    run_pairs(table, force, masks, partners, alive, 128, 320, scratch)
    own_force[...] = force[0:64]
    for c in range(6):
        even_force[c] = force[64:160, c, :]
        odd_force[c] = force[160:256, c, :]


def shape(*dims):
    return jax.ShapeDtypeStruct(dims, jnp.float32)


def own_pairs(part, partners, alive, state, masks, start):
    return pl.pallas_call(
        functools.partial(own_kernel, part),
        out_shape=shape(64, 8, TILE),
        in_specs=[SMEM, SMEM, VMEM, VMEM, VMEM],
        out_specs=VMEM,
        scratch_shapes=pair_scratch(64),
        compiler_params=params(),
        cost_estimate=cost(60_000_000, 2_000_000),
        name="own_pairs",
    )(partners, alive, state, masks, start)


def face_pairs(partners, alive, state, masks, ghost, start):
    return pl.pallas_call(
        face_kernel,
        out_shape=(shape(64, 8, TILE), shape(64, 8, TILE)),
        in_specs=[SMEM, SMEM, VMEM, VMEM, VMEM, VMEM],
        out_specs=(VMEM, VMEM),
        scratch_shapes=pair_scratch(128),
        compiler_params=params(),
        cost_estimate=cost(60_000_000, 2_000_000),
        name="face_pairs",
    )(partners, alive, state, masks, ghost, start)


def far_pairs(partners, alive, state, masks, even, odd, start):
    return pl.pallas_call(
        far_kernel,
        out_shape=(shape(64, 8, TILE), shape(6, 96, TILE), shape(6, 96, TILE)),
        in_specs=[SMEM, SMEM, VMEM, VMEM, VMEM, VMEM, VMEM],
        out_specs=(VMEM, VMEM, VMEM),
        scratch_shapes=pair_scratch(256),
        compiler_params=params(),
        cost_estimate=cost(200_000_000, 2_000_000),
        name="far_pairs",
    )(partners, alive, state, masks, even, odd, start)


def pick_kernel(rows, lists, own, near, next_, even, odd, ghost):
    sources = (own, near, next_)

    def one(e, carry):
        for which in range(3):
            tile = lists[which * 32 + e]
            even[:, pl.ds(which * 32 + e, 1), :] = sources[which][0:rows, pl.ds(tile, 1), :]
            tile = lists[96 + which * 32 + e]
            odd[:, pl.ds(which * 32 + e, 1), :] = sources[which][0:rows, pl.ds(tile, 1), :]
        for which in range(2):
            tile = lists[192 + which * 32 + e]
            ghost[:, pl.ds(which * 32 + e, 1), :] = sources[1 + which][0:rows, pl.ds(tile, 1), :]
        return carry

    lax.fori_loop(0, 32, one, 0)


def pick(rows, lists, own, near, next_):
    return pl.pallas_call(
        functools.partial(pick_kernel, rows),
        out_shape=(shape(rows, 96, TILE), shape(rows, 96, TILE), shape(rows, 64, TILE)),
        in_specs=[SMEM, VMEM, VMEM, VMEM],
        out_specs=(VMEM, VMEM, VMEM),
        compiler_params=params(),
        cost_estimate=cost(1_000_000, 3_000_000),
        name="pick",
    )(lists, own, near, next_)


def gather_kernel(lists, own, ghost, even, odd, own_total, near, next_, acc):
    acc[0:64] = own[...]
    acc[64:192] = jnp.zeros((128, 8, TILE), jnp.float32)

    def add(place, value):
        acc[place, 0:6] = acc[place, 0:6] + value

    def one(e, carry):
        for which in range(3):
            tile = lists[which * 32 + e] + which * 64
            add(tile, even[:, pl.ds(which * 32 + e, 1), :].reshape(6, TILE))
            tile = lists[96 + which * 32 + e] + which * 64
            add(tile, odd[:, pl.ds(which * 32 + e, 1), :].reshape(6, TILE))
        for which in range(2):
            tile = lists[192 + which * 32 + e] + (1 + which) * 64
            acc[tile] = acc[tile] + ghost[which * 32 + e]
        return carry

    lax.fori_loop(0, 32, one, 0)
    for c in range(6):
        own_total[c] = acc[0:64, c, :]
        near[c] = acc[64:128, c, :]
        next_[c] = acc[128:192, c, :]


def gather(lists, own, ghost, even, odd):
    return pl.pallas_call(
        gather_kernel,
        out_shape=(shape(6, 64, TILE),) * 3,
        in_specs=[SMEM, VMEM, VMEM, VMEM, VMEM],
        out_specs=(VMEM,) * 3,
        scratch_shapes=[pltpu.VMEM((192, 8, TILE), jnp.float32)],
        compiler_params=params(),
        cost_estimate=cost(1_000_000, 3_000_000),
        name="gather",
    )(lists, own, ghost, even, odd)


def push(record, moved):
    live = (record[9:10] > 0.0).astype(jnp.float32)
    position = record[0:3] + time_step * live * moved[0:3]
    return jnp.concatenate([position, moved, record[9:10]], axis=0)


def local(positions, velocities, spins, radii, counts, exports, partners, masks):
    tiles = radii.shape[-1] // TILE
    count = counts[0, 0]
    index = jnp.arange(tiles * TILE, dtype=jnp.int32)
    alive_sphere = (index < count).reshape(1, tiles, TILE)
    live = alive_sphere.astype(jnp.float32)
    radius = radii[0, 0].reshape(1, tiles, TILE)
    position = positions[0, 0].reshape(3, tiles, TILE)
    velocity = velocities[0, 0].reshape(3, tiles, TILE)
    spin = spins[0, 0].reshape(3, tiles, TILE)
    chosen = exports[0, 0]
    words = masks[0, 0]
    mass = mass_scale * radius * radius * radius
    inertia = 0.4 * mass * radius * radius
    lift = jnp.array([0.0, 0.0, -gravity], jnp.float32)[:, None, None]

    odd_x = lax.rem(lax.axis_index("gx"), 2)
    odd_y = lax.rem(lax.axis_index("gy"), 2)
    east = {0: odd_x == 1, 1: odd_x == 0}
    north = {0: odd_y == 0, 1: odd_y == 1}

    def choose(table, which):
        return lax.dynamic_index_in_dim(table, which, 0, keepdims=False)

    def face(a):
        return jnp.where(a, 0, 1)

    def side(b):
        return jnp.where(b, 2, 3)

    def corner(a, b):
        return jnp.where(a, jnp.where(b, 4, 5), jnp.where(b, 6, 7))

    state = jnp.concatenate(
        [position, velocity, spin, jnp.where(alive_sphere, radius, DEAD)], axis=0
    ).reshape(10, tiles, TILE)
    extra = jnp.concatenate(
        [chosen.reshape(2, TILE).astype(jnp.float32), jnp.zeros((6, TILE), jnp.float32)]
    )
    packed = jnp.concatenate([state.reshape(10 * tiles, TILE), extra])

    west_at = jnp.where(odd_x == 1, 0, 1)
    south_at = jnp.where(odd_y == 1, 0, 1)
    x_of = (west_at, 1 - west_at)
    y_of = (south_at, 1 - south_at)
    block_of = [
        x_of[0],
        x_of[1],
        2 + 3 * y_of[0],
        2 + 3 * y_of[1],
        3 + 3 * y_of[0] + x_of[0],
        3 + 3 * y_of[1] + x_of[0],
        3 + 3 * y_of[0] + x_of[1],
        3 + 3 * y_of[1] + x_of[1],
    ]
    block_of = jnp.stack(block_of).astype(jnp.int32)
    listed = partners[0, 0]
    kind = jnp.maximum(listed - tiles, 0) // 32
    hot = (kind[:, None] == jnp.arange(8, dtype=jnp.int32)[None, :]).astype(jnp.int32)
    slots = jnp.where(
        listed < tiles,
        listed,
        tiles + 32 * jnp.sum(hot * block_of[None, :], axis=1) + lax.rem(jnp.maximum(listed - tiles, 0), 32),
    )
    own_alive = (jnp.arange(tiles, dtype=jnp.int32) * TILE < count).astype(jnp.int32)

    shift_x = jnp.where(jnp.stack([east[0], east[1]]), -column_width, column_width)
    shift_y = jnp.where(jnp.stack([odd_y == 0, odd_y == 1]), column_width, -column_width)

    def shifted(record, dx, dy):
        moved = jnp.stack([dx, dy, jnp.zeros_like(dx)]).astype(jnp.float32)
        moved = jnp.repeat(moved, 32, axis=1)[:, :, None]
        return jnp.concatenate([record[0:3] + moved, record[3:]], axis=0)

    zero = jnp.zeros((), jnp.float32)
    face_dx, face_dy = shift_x, jnp.zeros((2,), jnp.float32)
    even_dx = jnp.stack([zero, shift_x[0], shift_x[1]])

    nothing = jnp.zeros((tiles, 8, TILE), jnp.float32)

    for step in range(STEPS):
        if step == 0:
            got_y = swap(packed, "gx", 1)
            got_x = swap(packed, "gx", 0)
            own_force = own_pairs((0, 3, 12), slots, own_alive, state, words, nothing)
            got_x, got_y, own_force = lax.optimization_barrier((got_x, got_y, own_force))
            near = got_x[: 10 * tiles].reshape(10, tiles, TILE)
            next_ = got_y[: 10 * tiles].reshape(10, tiles, TILE)
            list_x = got_x[10 * tiles : 10 * tiles + 2].astype(jnp.int32).reshape(8, 32)
            list_y = got_y[10 * tiles : 10 * tiles + 2].astype(jnp.int32).reshape(8, 32)
            lists = jnp.stack(
                [
                    choose(chosen, side(north[0])),
                    choose(list_x, corner(east[0], north[0])),
                    choose(list_y, corner(east[1], north[0])),
                    choose(chosen, side(north[1])),
                    choose(list_x, corner(east[0], north[1])),
                    choose(list_y, corner(east[1], north[1])),
                    choose(list_x, face(east[0])),
                    choose(list_y, face(east[1])),
                ]
            ).reshape(256)
            to_even, to_odd, ghost = pick(10, lists, state, near, next_)
            from_odd = swap(to_odd, "gy", 1)
            from_even = swap(to_even, "gy", 0)
            ghost = shifted(ghost, face_dx, face_dy)
            face_alive = (ghost[9, :, 0] > 0.0).astype(jnp.int32)
            alive = jnp.concatenate([own_alive, face_alive])
            own_force, ghost_force = face_pairs(slots, alive, state, words, ghost, own_force)
            from_even, from_odd, own_force = lax.optimization_barrier((from_even, from_odd, own_force))
            even = shifted(from_even, even_dx, jnp.broadcast_to(shift_y[0], (3,)))
            odd = shifted(from_odd, even_dx, jnp.broadcast_to(shift_y[1], (3,)))
            far = (jnp.concatenate([even[9, :, 0], odd[9, :, 0]]) > 0.0).astype(jnp.int32)
            alive = jnp.concatenate([alive, far])
        else:
            new = jnp.concatenate([velocity, spin], axis=0)
            got_y = swap(new, "gx", 1)
            got_x = swap(new, "gx", 0)
            own_force = own_pairs((0, 3, 12), slots, own_alive, state, words, nothing)
            got_x, got_y, own_force = lax.optimization_barrier((got_x, got_y, own_force))
            to_even, to_odd, ghost_new = pick(6, lists, new, got_x, got_y)
            from_odd = swap(to_odd, "gy", 1)
            from_even = swap(to_even, "gy", 0)
            ghost = push(ghost, ghost_new)
            own_force, ghost_force = face_pairs(slots, alive, state, words, ghost, own_force)
            from_even, from_odd, own_force = lax.optimization_barrier((from_even, from_odd, own_force))
            even = push(even, from_even)
            odd = push(odd, from_odd)
        own_force, even_force, odd_force = far_pairs(slots, alive, state, words, even, odd, own_force)
        back_odd = swap(odd_force, "gy", 1)
        back_even = swap(even_force, "gy", 0)
        own_force = own_pairs((3, 7, 12), slots, own_alive, state, words, own_force)
        back_odd, back_even, own_force = lax.optimization_barrier((back_odd, back_even, own_force))
        own_total, to_x, to_y = gather(lists, own_force, ghost_force, back_even, back_odd)
        back_y = swap(to_y, "gx", 1)
        back_x = swap(to_x, "gx", 0)
        own_total, later = lax.optimization_barrier((own_total, nothing))
        last_force = own_pairs((7, 12, 12), slots, own_alive, state, words, later)
        last_force = jnp.transpose(last_force, (1, 0, 2))[0:6]
        force = own_total + last_force + back_x + back_y
        velocity = velocity + time_step * live * (force[0:3] / mass + lift)
        spin = spin + time_step * live * force[3:6] / inertia
        position = position + time_step * live * velocity
        state = jnp.concatenate([position, velocity, spin, state[9:10]], axis=0)
    result = (1, 1, 3, tiles * TILE)
    return (position.reshape(result), velocity.reshape(result), spin.reshape(result))


def solution(mesh):
    return jax.shard_map(
        local,
        mesh=mesh,
        in_specs=(
            P("gx", "gy", None, None),
            P("gx", "gy", None, None),
            P("gx", "gy", None, None),
            P("gx", "gy", None),
            P("gx", "gy"),
            P("gx", "gy", None, None),
            P("gx", "gy", None),
            P("gx", "gy", None, None, None),
        ),
        out_specs=(P("gx", "gy", None, None), P("gx", "gy", None, None), P("gx", "gy", None, None)),
        check_vma=False,
    )
```

```python
import functools

import jax
import jax.numpy as jnp
from jax import lax
from jax.experimental import pallas as pl
from jax.experimental.pallas import tpu as pltpu
from jax.sharding import PartitionSpec as P

TILE = 128
STEPS = 2
SECOND_PARTS = ((0, 5, 12), (5, 12, 12))
BLOCK = 32
UNROLL = 2

stiffness = 1.0
damping_normal = 0.5
damping_tangent = 0.3
softening = 0.05
time_step = 0.25
column_width = 3.0
gravity = 1.0
mass_scale = 8.0

DEAD = -10.0

VMEM = pl.BlockSpec(memory_space=pltpu.VMEM)
SMEM = pl.BlockSpec(memory_space=pltpu.SMEM)
VMEM_LIMIT = 20 * 1024 * 1024


def swap(value, axis, odd):
    count = lax.axis_size(axis)
    pairs = []
    for i in range(odd, count, 2):
        k = (i + 1) % count
        pairs += [(i, k), (k, i)]
    return lax.ppermute(value, axis, pairs)


def params():
    return pltpu.CompilerParams(vmem_limit_bytes=VMEM_LIMIT)


def cost(flops, size):
    return pl.CostEstimate(flops=flops, bytes_accessed=size, transcendentals=0)


def cross(a, b):
    return (
        a[1] * b[2] - a[2] * b[1],
        a[2] * b[0] - a[0] * b[2],
        a[0] * b[1] - a[1] * b[0],
    )


FIELDS = 11


def split(value):
    high = value.astype(jnp.bfloat16).astype(jnp.float32)
    rest = value - high
    middle = rest.astype(jnp.bfloat16).astype(jnp.float32)
    return high, middle, rest - middle


def fill_constants(spread, sums):
    sub = lax.broadcasted_iota(jnp.int32, (64, TILE), 0)
    for c in range(FIELDS):
        here = (lax.rem(sub, 16) == min(c, 9)) & (sub < 48)
        for ref in spread:
            ref[:, c * TILE : (c + 1) * TILE] = here.astype(jnp.float32).astype(jnp.bfloat16)
    row = lax.broadcasted_iota(jnp.int32, (16, 6 * TILE), 0)
    column = lax.rem(lax.broadcasted_iota(jnp.int32, (16, 6 * TILE), 1) // (TILE // 2), 6)
    sums[...] = (row == column).astype(jnp.float32).astype(jnp.bfloat16)


def combine(rec_i, rec_j, spread, both):
    high, middle, low = split(rec_i)
    sub = lax.broadcasted_iota(jnp.int32, (16, TILE), 0)
    for c in range(10):
        rows = jnp.where(
            sub == 0,
            high[c : c + 1],
            jnp.where(sub == 1, middle[c : c + 1], jnp.where(sub == 2, low[c : c + 1], 0.0)),
        )
        if c < 6:
            rows = -rows
        spread[48:64, c * TILE : (c + 1) * TILE] = rows.astype(jnp.bfloat16)
    high, middle, low = split(rec_j)
    left = jnp.concatenate(
        [high, middle, low, jnp.ones((16, TILE), jnp.float32), jnp.zeros((64, TILE), jnp.float32)], axis=0
    )
    left = jnp.transpose(left)[:, 0:64].astype(jnp.bfloat16)
    both[...] = jnp.dot(left, spread[...], preferred_element_type=jnp.float32)


def fold(first, second):
    low = lax.broadcasted_iota(jnp.int32, first.shape, 1) < TILE // 2
    kept = jnp.where(low, first, second)
    other = jnp.where(low, second, first)
    return kept + pltpu.roll(other, TILE // 2, 1)


def pair_forces(rec_i, words, both, parts):
    radius_i = rec_i[9:10, :]
    scaled = damping_tangent * damping_tangent * radius_i
    sub = lax.broadcasted_iota(jnp.int32, (8, TILE), 0)
    bit = jnp.left_shift(1, sub)
    sums_i = [jnp.zeros((8, TILE), jnp.float32) for _ in range(6)]
    for first in range(0, TILE, BLOCK):
        field = [both[first : first + BLOCK, c * TILE : (c + 1) * TILE] for c in range(FIELDS)]
        r, dv, spin = field[0:3], field[3:6], field[6:9]
        d2 = r[0] * r[0] + r[1] * r[1] + (r[2] * r[2] + softening * softening)
        inv = lax.rsqrt(d2)
        inter = jnp.maximum(field[9] - d2 * inv, 0.0)
        top = field[10] * scaled * inter
        root = top * lax.rsqrt(jnp.maximum(top * field[9], 1e-30))
        hit = jnp.concatenate(
            [
                (jnp.broadcast_to(words[w : w + 1, :], (8, TILE)) & bit) != 0
                for w in range(first // 8, (first + BLOCK) // 8)
            ],
            axis=0,
        )
        k2 = jnp.where(hit, root, 0.0)
        n = [inv * x for x in r]
        speed_n = dv[0] * n[0] + dv[1] * n[1] + dv[2] * n[2]
        k1 = k2 * (
            (stiffness / damping_tangent) * inter
            - ((damping_normal - damping_tangent) / damping_tangent) * speed_n
        )
        turn = cross(spin, n)
        drag = [k2 * (dv[c] - turn[c]) for c in range(3)]
        terms = [drag[c] - k1 * n[c] for c in range(3)] + list(cross(n, drag))
        for c in range(6):
            part = terms[c]
            sums_i[c] = sums_i[c] + sum(part[8 * q : 8 * q + 8] for q in range(BLOCK // 8))
        for c in range(3):
            part = fold(terms[2 * c], terms[2 * c + 1])
            high = part.astype(jnp.bfloat16)
            low = (part - high.astype(jnp.float32)).astype(jnp.bfloat16)
            parts[first : first + BLOCK, c * TILE : (c + 1) * TILE] = high
            parts[first : first + BLOCK, (3 + c) * TILE : (4 + c) * TILE] = low
    own = jnp.zeros((8, TILE), jnp.float32)
    for c in range(6):
        own = jnp.where(sub == c, jnp.sum(sums_i[c], axis=0, keepdims=True), own)
    own = own * jnp.where(sub < 3, 1.0, radius_i)
    return own


def forces_back(rec_j, parts, sums):
    over = (((1,), (1,)), ((), ()))
    back = lax.dot_general(sums[...], parts[...], over, preferred_element_type=jnp.float32)
    sub = lax.broadcasted_iota(jnp.int32, (8, TILE), 0)
    return back[0:8] * jnp.where(sub < 3, -1.0, rec_j[9:10, :])


def load_tiles(table, first, number, record, moved=None, shifts=()):
    def rows(ref, c):
        return ref[c * number : (c + 1) * number, :]

    radius = rows(record, 9)
    live = jnp.where(radius > 0.0, 1.0, 0.0)
    for c in range(10):
        if c == 9:
            value = radius
        elif moved is None:
            value = rows(record, c)
        elif c < 3:
            value = rows(record, c) + time_step * live * rows(moved, c)
        else:
            value = rows(moved, c - 3)
        if 6 <= c < 9:
            value = value * radius
        if c < 2 and shifts:
            value = jnp.concatenate([value[32 * k : 32 * k + 32] + at[c] for k, at in enumerate(shifts)], axis=0)
        table[pl.ds(first * 16 + c, number, stride=16), :] = value


def run_pairs(table, force, masks, chosen, partners, skipped, scratch, part):
    spread, both, parts = (scratch[k * UNROLL : (k + 1) * UNROLL] for k in range(3))
    sums = scratch[3 * UNROLL]
    fill_constants(spread, sums)
    last = force.shape[0] // 8 - 1
    table[last * 16 : last * 16 + 16] = jnp.full((16, TILE), DEAD, jnp.float32)
    force[last * 8 : last * 8 + 8] = jnp.zeros((8, TILE), jnp.float32)

    found = chosen[128]
    origin, number = found * part[0] // part[2], found * part[1] // part[2]

    def entry(n):
        real = n + origin < number
        p = jnp.where(real, chosen[jnp.minimum(n + origin, 127)], 0)
        owner = jnp.where(real, p // 2, last)
        place = jnp.where(real, partners[p] - skipped, last)
        return p, owner, place

    def record(tile):
        return table[pl.ds(pl.multiple_of(tile * 16, 16), 16), :]

    def prepare(item, spread, both):
        combine(record(item[1]), record(item[2]), spread, both)

    def forces(item, both, parts):
        return pair_forces(record(item[1]), masks[item[0]], both, parts)

    def back(place, parts):
        return forces_back(record(place), parts, sums)

    def add(tile, value):
        at = pl.ds(pl.multiple_of(tile * 8, 8), 8)
        force[at, :] = force[at, :] + value

    parts[-1][...] = jnp.zeros_like(parts[-1])
    prepare(entry(0), spread[0], both[0])

    def some(t, before):
        items = [entry(UNROLL * t + k) for k in range(UNROLL + 1)]
        results = []
        place = before
        for k in range(UNROLL):
            after = (k + 1) % UNROLL
            prepare(items[k + 1], spread[after], both[after])
            results.append((place, back(place, parts[k - 1])))
            results.append((items[k][1], forces(items[k], both[k], parts[k])))
            place = items[k][2]
        for tile, value in results:
            add(tile, value)
        return place

    final = lax.fori_loop(0, (number - origin + UNROLL - 1) // UNROLL, some, jnp.int32(last))
    add(final, back(final, parts[-1]))


def pair_scratch(tiles):
    return [
        pltpu.VMEM(((tiles + 1) * 16, TILE), jnp.float32),
        pltpu.VMEM(((tiles + 1) * 8, TILE), jnp.float32),
        *[pltpu.VMEM((64, FIELDS * TILE), jnp.bfloat16)] * UNROLL,
        *[pltpu.VMEM((TILE, FIELDS * TILE), jnp.float32)] * UNROLL,
        *[pltpu.VMEM((TILE, 6 * TILE), jnp.bfloat16)] * UNROLL,
        pltpu.VMEM((16, 6 * TILE), jnp.bfloat16),
    ]


def scan(low, high, partners, alive, chosen):
    def some(block, found):
        pairs = [block * 16 + k for k in range(16)]
        slots = [partners[p] for p in pairs]
        owners = [alive[block * 8 + k] for k in range(8)]
        others = [alive[slot] for slot in slots]
        for k in range(16):
            good = (slots[k] >= low) & (slots[k] < high) & (owners[k // 2] + others[k] == 2)
            chosen[found] = pairs[k]
            found = found + good.astype(jnp.int32)
        return found

    chosen[128] = lax.fori_loop(0, 8, some, 0)


def by_field(target, force, first, number, at=0):
    width = target.shape[0] // 6
    for c in range(6):
        rows = force[pl.ds(first * 8 + c, number, stride=8), :]
        target[c * width + at : c * width + at + number, :] = rows


def pairs_kernel(kind, part, listed, pushed, *refs):
    refs = list(refs)
    partners, chosen, shift, masks, start = (refs.pop(0) for _ in range(5))
    sides = [refs.pop(0) for _ in range(2)] if kind == "far" else ()
    ghosts = {"own": 0, "x": 1, "y": 2, "far": 2}[kind]
    records = [refs.pop(0) for _ in range(1 + ghosts)]
    moved = [refs.pop(0) for _ in range(1 + ghosts)] if pushed else [None] * (1 + ghosts)
    number = 0 if kind == "own" else 32 if kind == "y" else 64
    low = {"own": 0, "x": 64, "y": 128, "far": 192}[kind]
    own_force = refs.pop(0)
    outs = [refs.pop(0) for _ in range(ghosts)]
    if not listed:
        alive, chosen = chosen, refs.pop(0)
        scan(low, low + ghosts * number if ghosts else 64, partners, alive, chosen)
    table, force, *scratch = refs
    tiles = 64 + ghosts * number
    table[...] = jnp.zeros_like(table)
    load_tiles(table, 0, 64, records[0], moved[0])
    for k in range(ghosts):
        if kind == "x":
            shifts = ((shift[0], 0.0), (shift[1], 0.0))
        elif kind == "y":
            shifts = ((0.0, shift[2 + k]),)
        else:
            shifts = ((shift[0], shift[2 + k]), (shift[1], shift[2 + k]))
        load_tiles(table, 64 + k * number, number, records[1 + k], moved[1 + k], shifts)
    force[0:512] = start[...]
    if ghosts:
        force[512 : tiles * 8] = jnp.zeros((tiles * 8 - 512, TILE), jnp.float32)
    run_pairs(table, force, masks, chosen, partners, max(low - 64, 0), scratch, part)
    if own_force.shape[0] == 384:
        by_field(own_force, force, 0, 64)
    else:
        own_force[...] = force[0:512]
    for k in range(ghosts):
        if kind == "x":
            outs[k][...] = force[512:1024]
        elif kind == "y":
            by_field(outs[k], force, 64 + 32 * k, 32)
        else:
            for c in range(6):
                outs[k][c * 96 : c * 96 + 32, :] = sides[k][c * 32 : (c + 1) * 32, :]
            by_field(outs[k], force, 64 + 64 * k, 64, 32)


def shape(*dims):
    return jax.ShapeDtypeStruct(dims, jnp.float32)


def pairs(kind, partners, listing, shift, masks, start, records, moved=(), sides=(), part=(0, 1, 1), last=False):
    listed = listing.shape[0] == 136
    outs = {"own": [], "x": [512], "y": [192, 192], "far": [576, 576]}[kind]
    shapes = [shape(rows, TILE) for rows in [384 if last else 512] + outs]
    places = [VMEM] * len(shapes)
    if not listed:
        shapes.append(jax.ShapeDtypeStruct((136,), jnp.int32))
        places.append(SMEM)
    return pl.pallas_call(
        functools.partial(pairs_kernel, kind, part, listed, bool(moved)),
        out_shape=shapes,
        in_specs=[SMEM] * 3 + [VMEM] * (2 + len(sides) + len(records) + len(moved)),
        out_specs=places,
        scratch_shapes=pair_scratch({"own": 64, "x": 128, "y": 128, "far": 192}[kind]),
        compiler_params=params(),
        cost_estimate=cost(60_000_000, 2_000_000),
        name=kind + "_pairs",
    )(partners, listing, shift, masks, start, *sides, *records, *moved)


def copy_tile(rows, source, tile, target, place, width):
    target[pl.ds(place, rows, stride=width), :] = source[pl.ds(tile, rows, stride=64), :]


def pick_own_kernel(rows, lists, own, even, odd):
    def some(block, carry):
        for k in range(4):
            e = block * 4 + k
            copy_tile(rows, own, lists[e], even, e, 32)
            copy_tile(rows, own, lists[96 + e], odd, e, 32)
        return carry

    lax.fori_loop(0, 8, some, 0)


def pick_kernel(rows, lists, near, next_, even, odd, ghost):
    sources = (near, next_)

    def some(block, carry):
        for k in range(4):
            e = block * 4 + k
            for which in range(2):
                place = which * 32 + e
                copy_tile(rows, sources[which], lists[32 + place], even, place, 64)
                copy_tile(rows, sources[which], lists[128 + place], odd, place, 64)
                copy_tile(rows, sources[which], lists[192 + place], ghost, place, 64)
        return carry

    lax.fori_loop(0, 8, some, 0)


def pick_own(rows, lists, own):
    return pl.pallas_call(
        functools.partial(pick_own_kernel, rows),
        out_shape=(shape(rows * 32, TILE),) * 2,
        in_specs=[SMEM, VMEM],
        out_specs=(VMEM,) * 2,
        compiler_params=params(),
        cost_estimate=cost(1_000_000, 1_000_000),
        name="pick_own",
    )(lists, own)


def pick(rows, lists, near, next_):
    return pl.pallas_call(
        functools.partial(pick_kernel, rows),
        out_shape=(shape(rows * 64, TILE),) * 3,
        in_specs=[SMEM, VMEM, VMEM],
        out_specs=(VMEM,) * 3,
        compiler_params=params(),
        cost_estimate=cost(1_000_000, 3_000_000),
        name="pick",
    )(lists, near, next_)


def gather_kernel(lists, ghost, even, odd, own_total, near, next_, acc):
    acc[...] = jnp.zeros_like(acc)

    def add(tile, value):
        at = pl.ds(pl.multiple_of(tile * 8, 8), value.shape[0])
        acc[at, :] = acc[at, :] + value

    def some(block, carry):
        for k in range(4):
            e = block * 4 + k
            for which in range(3):
                add(lists[which * 32 + e] + which * 64, even[pl.ds(which * 32 + e, 6, stride=96), :])
                add(lists[96 + which * 32 + e] + which * 64, odd[pl.ds(which * 32 + e, 6, stride=96), :])
            for which in range(2):
                place = which * 32 + e
                value = ghost[pl.ds(pl.multiple_of(place * 8, 8), 8), :]
                add(lists[192 + place] + (1 + which) * 64, value)
        return carry

    lax.fori_loop(0, 8, some, 0)
    for k, total in enumerate((own_total, near, next_)):
        by_field(total, acc, 64 * k, 64)


def gather(lists, ghost, even, odd):
    return pl.pallas_call(
        gather_kernel,
        out_shape=(shape(384, TILE),) * 3,
        in_specs=[SMEM, VMEM, VMEM, VMEM],
        out_specs=(VMEM,) * 3,
        scratch_shapes=[pltpu.VMEM((1536, TILE), jnp.float32)],
        compiler_params=params(),
        cost_estimate=cost(1_000_000, 3_000_000),
        name="gather",
    )(lists, ghost, even, odd)


def local(positions, velocities, spins, radii, counts, exports, partners, masks):
    tiles = radii.shape[-1] // TILE
    count = counts[0, 0]
    index = jnp.arange(tiles * TILE, dtype=jnp.int32)
    alive_sphere = (index < count).reshape(1, tiles, TILE)
    live = alive_sphere.astype(jnp.float32)
    radius = radii[0, 0].reshape(1, tiles, TILE)
    position = positions[0, 0].reshape(3, tiles, TILE)
    velocity = velocities[0, 0].reshape(3, tiles, TILE)
    spin = spins[0, 0].reshape(3, tiles, TILE)
    chosen = exports[0, 0]
    words = masks[0, 0]
    mass = mass_scale * radius * radius * radius
    inertia = 0.4 * mass * radius * radius
    lift = jnp.array([0.0, 0.0, -gravity], jnp.float32)[:, None, None]

    odd_x = lax.rem(lax.axis_index("gx"), 2)
    odd_y = lax.rem(lax.axis_index("gy"), 2)
    east = {0: odd_x == 1, 1: odd_x == 0}
    north = {0: odd_y == 0, 1: odd_y == 1}

    def choose(table, which):
        return lax.dynamic_index_in_dim(table, which, 0, keepdims=False)

    def face(a):
        return jnp.where(a, 0, 1)

    def side(b):
        return jnp.where(b, 2, 3)

    def corner(a, b):
        return jnp.where(a, jnp.where(b, 4, 5), jnp.where(b, 6, 7))

    state = jnp.concatenate(
        [position, velocity, spin, jnp.where(alive_sphere, radius, DEAD)], axis=0
    ).reshape(10 * tiles, TILE)
    extra = jnp.concatenate(
        [chosen.reshape(2, TILE).astype(jnp.float32), jnp.zeros((6, TILE), jnp.float32)]
    )
    packed = jnp.concatenate([state, extra])
    got_y = swap(packed, "gx", 1)
    got_x = swap(packed, "gx", 0)

    west_at = jnp.where(odd_x == 1, 0, 1)
    south_at = jnp.where(odd_y == 1, 0, 1)
    x_of = (west_at, 1 - west_at)
    y_of = (south_at, 1 - south_at)
    block_of = [
        x_of[0],
        x_of[1],
        2 + y_of[0],
        2 + y_of[1],
        4 + 2 * y_of[0] + x_of[0],
        4 + 2 * y_of[1] + x_of[0],
        4 + 2 * y_of[0] + x_of[1],
        4 + 2 * y_of[1] + x_of[1],
    ]
    block_of = jnp.stack(block_of).astype(jnp.int32)
    listed = partners[0, 0]
    kind = jnp.maximum(listed - tiles, 0) // 32
    hot = (kind[:, None] == jnp.arange(8, dtype=jnp.int32)[None, :]).astype(jnp.int32)
    slots = jnp.where(
        listed < tiles,
        listed,
        tiles + 32 * jnp.sum(hot * block_of[None, :], axis=1) + lax.rem(jnp.maximum(listed - tiles, 0), 32),
    )
    own_alive = (jnp.arange(tiles, dtype=jnp.int32) * TILE < count).astype(jnp.int32)

    shift = jnp.stack(
        [
            jnp.where(east[0], -column_width, column_width),
            jnp.where(east[1], -column_width, column_width),
            jnp.where(north[0], column_width, -column_width),
            jnp.where(north[1], column_width, -column_width),
        ]
    ).astype(jnp.float32)
    nothing = jnp.zeros((tiles * 8, TILE), jnp.float32)

    def alive_in(record):
        return (record[9 * record.shape[0] // 10 :, 0] > 0.0).astype(jnp.int32)

    def exchange_sides(rows, lists, own):
        to_even, to_odd = pick_own(rows, lists, own)
        return swap(to_even, "gy", 0), swap(to_odd, "gy", 1)

    own_lists = [choose(chosen, side(north[0])), choose(chosen, side(north[1]))]

    for step in range(STEPS):
        if step == 0:
            blank = jnp.zeros((64,), jnp.int32)
            lists = jnp.concatenate([own_lists[0], blank, own_lists[1], blank, blank])
            even_side, odd_side = exchange_sides(10, lists, state)
            list_x = got_x[10 * tiles : 10 * tiles + 2].astype(jnp.int32).reshape(8, 32)
            list_y = got_y[10 * tiles : 10 * tiles + 2].astype(jnp.int32).reshape(8, 32)
            lists = jnp.stack(
                [
                    own_lists[0],
                    choose(list_x, corner(east[0], north[0])),
                    choose(list_y, corner(east[1], north[0])),
                    own_lists[1],
                    choose(list_x, corner(east[0], north[1])),
                    choose(list_y, corner(east[1], north[1])),
                    choose(list_x, face(east[0])),
                    choose(list_y, face(east[1])),
                ]
            ).reshape(256)
            to_even, to_odd, ghost = pick(10, lists, got_x, got_y)
            even, odd = swap(to_even, "gy", 0), swap(to_odd, "gy", 1)
            alive = jnp.concatenate([own_alive, alive_in(ghost), alive_in(even_side), alive_in(odd_side)])
            near_alive = jnp.concatenate([alive, jnp.zeros((128,), jnp.int32)])
            own_force, *sides, y_list = pairs(
                "y", slots, near_alive, shift, words, nothing, (state, even_side, odd_side)
            )
            even, odd, own_force = lax.optimization_barrier((even, odd, own_force))
            far_alive = jnp.concatenate([alive, alive_in(even), alive_in(odd)])
            own_force, even_force, odd_force, far_list = pairs(
                "far", slots, far_alive, shift, words, own_force, (state, even, odd), (), sides
            )
            back_even, back_odd = swap(even_force, "gy", 0), swap(odd_force, "gy", 1)
            own_force, ghost_force, x_list = pairs("x", slots, near_alive, shift, words, own_force, (state, ghost))
        else:
            new = jnp.concatenate([velocity, spin], axis=0).reshape(6 * tiles, TILE)
            got_y = swap(new, "gx", 1)
            got_x = swap(new, "gx", 0)
            to_even, to_odd = pick_own(6, lists, new)
            even_side_new, odd_side_new = swap(to_even, "gy", 0), swap(to_odd, "gy", 1)
            own_force, *sides = pairs(
                "y",
                slots,
                y_list,
                shift,
                words,
                nothing,
                (state, even_side, odd_side),
                (new, even_side_new, odd_side_new),
            )
            got_x, got_y, own_force = lax.optimization_barrier((got_x, got_y, own_force))
            to_even, to_odd, ghost_new = pick(6, lists, got_x, got_y)
            even_new, odd_new = swap(to_even, "gy", 0), swap(to_odd, "gy", 1)
            own_force, _ = lax.optimization_barrier((own_force, to_even))
            own_force = pairs(
                "own", slots, own_list, shift, words, own_force, (state,), (new,), part=SECOND_PARTS[0]
            )[0]
            even_new, odd_new, own_force = lax.optimization_barrier((even_new, odd_new, own_force))
            own_force, even_force, odd_force = pairs(
                "far", slots, far_list, shift, words, own_force, (state, even, odd), (new, even_new, odd_new), sides
            )
            back_even, back_odd = swap(even_force, "gy", 0), swap(odd_force, "gy", 1)
            own_force, ghost_force = pairs(
                "x", slots, x_list, shift, words, own_force, (state, ghost), (new, ghost_new)
            )
        back_odd, back_even, own_force = lax.optimization_barrier((back_odd, back_even, own_force))
        own_total, to_x, to_y = gather(lists, ghost_force, back_even, back_odd)
        back_y = swap(to_y, "gx", 1)
        back_x = swap(to_x, "gx", 0)
        own_total, own_force = lax.optimization_barrier((own_total, own_force))
        if step == 0:
            last_force, own_list = pairs("own", slots, near_alive, shift, words, own_force, (state,), last=True)
        else:
            (last_force,) = pairs(
                "own",
                slots,
                own_list,
                shift,
                words,
                own_force,
                (state,),
                (new,),
                part=SECOND_PARTS[1],
                last=True,
            )
        force = sum(part.reshape(6, tiles, TILE) for part in (own_total, back_x, back_y, last_force))
        velocity = velocity + time_step * live * (force[0:3] / mass + lift)
        spin = spin + time_step * live * force[3:6] / inertia
        position = position + time_step * live * velocity
    result = (1, 1, 3, tiles * TILE)
    return (position.reshape(result), velocity.reshape(result), spin.reshape(result))


def solution(mesh):
    return jax.shard_map(
        local,
        mesh=mesh,
        in_specs=(
            P("gx", "gy", None, None),
            P("gx", "gy", None, None),
            P("gx", "gy", None, None),
            P("gx", "gy", None),
            P("gx", "gy"),
            P("gx", "gy", None, None),
            P("gx", "gy", None),
            P("gx", "gy", None, None, None),
        ),
        out_specs=(P("gx", "gy", None, None), P("gx", "gy", None, None), P("gx", "gy", None, None)),
        check_vma=False,
    )
```

```python
import functools

import jax
import jax.numpy as jnp
from jax import lax
from jax.experimental import pallas as pl
from jax.experimental.pallas import tpu as pltpu
from jax.sharding import PartitionSpec as P

TILE = 128
STEPS = 2
BLOCK = 32
UNROLL = 2

stiffness = 1.0
damping_normal = 0.5
damping_tangent = 0.3
softening = 0.05
time_step = 0.25
column_width = 3.0
gravity = 1.0
mass_scale = 8.0

DEAD = -10.0

VMEM = pl.BlockSpec(memory_space=pltpu.VMEM)
SMEM = pl.BlockSpec(memory_space=pltpu.SMEM)
VMEM_LIMIT = 20 * 1024 * 1024


def swap(value, axis, odd):
    count = lax.axis_size(axis)
    pairs = []
    for i in range(odd, count, 2):
        k = (i + 1) % count
        pairs += [(i, k), (k, i)]
    return lax.ppermute(value, axis, pairs)


def params():
    return pltpu.CompilerParams(vmem_limit_bytes=VMEM_LIMIT)


def cost(flops, size):
    return pl.CostEstimate(flops=flops, bytes_accessed=size, transcendentals=0)


def cross(a, b):
    return (
        a[1] * b[2] - a[2] * b[1],
        a[2] * b[0] - a[0] * b[2],
        a[0] * b[1] - a[1] * b[0],
    )


FIELDS = 10


def split(value):
    high = value.astype(jnp.bfloat16).astype(jnp.float32)
    rest = value - high
    middle = rest.astype(jnp.bfloat16).astype(jnp.float32)
    return high, middle, rest - middle


def fill_constants(spread, sums):
    sub = lax.broadcasted_iota(jnp.int32, (64, TILE), 0)
    for c in range(FIELDS):
        here = (lax.rem(sub, 16) == c) & (sub < 48)
        for ref in spread:
            ref[:, c * TILE : (c + 1) * TILE] = here.astype(jnp.float32).astype(jnp.bfloat16)
    row = lax.broadcasted_iota(jnp.int32, (16, 6 * TILE), 0)
    column = lax.rem(lax.broadcasted_iota(jnp.int32, (16, 6 * TILE), 1) // (TILE // 2), 6)
    sums[...] = (row == column).astype(jnp.float32).astype(jnp.bfloat16)


def combine(rec_i, rec_j, spread, both):
    high, middle, low = split(rec_i)
    sub = lax.broadcasted_iota(jnp.int32, (16, TILE), 0)
    for c in range(10):
        rows = jnp.where(
            sub == 0,
            high[c : c + 1],
            jnp.where(sub == 1, middle[c : c + 1], jnp.where(sub == 2, low[c : c + 1], 0.0)),
        )
        if c < 6:
            rows = -rows
        spread[48:64, c * TILE : (c + 1) * TILE] = rows.astype(jnp.bfloat16)
    high, middle, low = split(rec_j)
    left = jnp.concatenate(
        [high, middle, low, jnp.ones((16, TILE), jnp.float32), jnp.zeros((64, TILE), jnp.float32)], axis=0
    )
    left = jnp.transpose(left)[:, 0:64].astype(jnp.bfloat16)
    both[...] = jnp.dot(left, spread[...], preferred_element_type=jnp.float32)


def fold(first, second):
    low = lax.broadcasted_iota(jnp.int32, first.shape, 1) < TILE // 2
    kept = jnp.where(low, first, second)
    other = jnp.where(low, second, first)
    return kept + pltpu.roll(other, TILE // 2, 1)


def pair_forces(rec_i, words, both, parts):
    radius_i = rec_i[9:10, :]
    scaled = damping_tangent * damping_tangent * radius_i
    sub = lax.broadcasted_iota(jnp.int32, (8, TILE), 0)
    bit = jnp.left_shift(1, sub)
    sums_i = [jnp.zeros((8, TILE), jnp.float32) for _ in range(6)]
    for first in range(0, TILE, BLOCK):
        field = [both[first : first + BLOCK, c * TILE : (c + 1) * TILE] for c in range(FIELDS)]
        r, dv, spin = field[0:3], field[3:6], field[6:9]
        d2 = r[0] * r[0] + r[1] * r[1] + (r[2] * r[2] + softening * softening)
        inv = lax.rsqrt(d2)
        inter = jnp.maximum(field[9] - d2 * inv, 0.0)
        top = (field[9] - radius_i) * scaled * inter
        root = top * lax.rsqrt(jnp.maximum(top * field[9], 1e-30))
        hit = jnp.concatenate(
            [
                (jnp.broadcast_to(words[w : w + 1, :], (8, TILE)) & bit) != 0
                for w in range(first // 8, (first + BLOCK) // 8)
            ],
            axis=0,
        )
        k2 = jnp.where(hit, root, 0.0)
        n = [inv * x for x in r]
        speed_n = dv[0] * n[0] + dv[1] * n[1] + dv[2] * n[2]
        k1 = k2 * (
            (stiffness / damping_tangent) * inter
            - ((damping_normal - damping_tangent) / damping_tangent) * speed_n
        )
        turn = cross(spin, n)
        drag = [k2 * (dv[c] - turn[c]) for c in range(3)]
        terms = [drag[c] - k1 * n[c] for c in range(3)] + list(cross(n, drag))
        for c in range(6):
            part = terms[c]
            sums_i[c] = sums_i[c] + sum(part[8 * q : 8 * q + 8] for q in range(BLOCK // 8))
        for c in range(3):
            part = fold(terms[2 * c], terms[2 * c + 1])
            high = part.astype(jnp.bfloat16)
            low = (part - high.astype(jnp.float32)).astype(jnp.bfloat16)
            parts[first : first + BLOCK, c * TILE : (c + 1) * TILE] = high
            parts[first : first + BLOCK, (3 + c) * TILE : (4 + c) * TILE] = low
    own = jnp.zeros((8, TILE), jnp.float32)
    for c in range(6):
        own = jnp.where(sub == c, jnp.sum(sums_i[c], axis=0, keepdims=True), own)
    own = own * jnp.where(sub < 3, 1.0, radius_i)
    return own


def forces_back(rec_j, parts, sums):
    over = (((1,), (1,)), ((), ()))
    back = lax.dot_general(sums[...], parts[...], over, preferred_element_type=jnp.float32)
    sub = lax.broadcasted_iota(jnp.int32, (8, TILE), 0)
    return back[0:8] * jnp.where(sub < 3, -1.0, rec_j[9:10, :])


def load_tiles(table, first, number, record, moved=None, shifts=()):
    def rows(ref, c):
        return ref[c * number : (c + 1) * number, :]

    radius = rows(record, 9)
    live = jnp.where(radius > 0.0, 1.0, 0.0)
    for c in range(10):
        if c == 9:
            value = radius
        elif moved is None:
            value = rows(record, c)
        elif c < 3:
            value = rows(record, c) + time_step * live * rows(moved, c)
        else:
            value = rows(moved, c - 3)
        if 6 <= c < 9:
            value = value * radius
        if c < 2 and shifts:
            value = jnp.concatenate([value[32 * k : 32 * k + 32] + at[c] for k, at in enumerate(shifts)], axis=0)
        table[pl.ds(first * 16 + c, number, stride=16), :] = value


def run_pairs(table, force, masks, chosen, partners, skipped, scratch):
    spread, both, parts = (scratch[k * UNROLL : (k + 1) * UNROLL] for k in range(3))
    sums = scratch[3 * UNROLL]
    fill_constants(spread, sums)
    last = force.shape[0] // 8 - 1
    table[last * 16 : last * 16 + 16] = jnp.full((16, TILE), DEAD, jnp.float32)
    force[last * 8 : last * 8 + 8] = jnp.zeros((8, TILE), jnp.float32)

    number = chosen[128]

    def entry(n):
        real = n < number
        p = jnp.where(real, chosen[jnp.minimum(n, 127)], 0)
        owner = jnp.where(real, p // 2, last)
        place = jnp.where(real, partners[p] - skipped, last)
        return p, owner, place

    def record(tile):
        return table[pl.ds(pl.multiple_of(tile * 16, 16), 16), :]

    def prepare(item, spread, both):
        combine(record(item[1]), record(item[2]), spread, both)

    def forces(item, both, parts):
        return pair_forces(record(item[1]), masks[item[0]], both, parts)

    def back(place, parts):
        return forces_back(record(place), parts, sums)

    def add(tile, value):
        at = pl.ds(pl.multiple_of(tile * 8, 8), 8)
        force[at, :] = force[at, :] + value

    parts[-1][...] = jnp.zeros_like(parts[-1])
    prepare(entry(0), spread[0], both[0])

    def some(t, before):
        items = [entry(UNROLL * t + k) for k in range(UNROLL + 1)]
        results = []
        place = before
        for k in range(UNROLL):
            after = (k + 1) % UNROLL
            prepare(items[k + 1], spread[after], both[after])
            results.append((place, back(place, parts[k - 1])))
            results.append((items[k][1], forces(items[k], both[k], parts[k])))
            place = items[k][2]
        for tile, value in results:
            add(tile, value)
        return place

    final = lax.fori_loop(0, (number + UNROLL - 1) // UNROLL, some, jnp.int32(last))
    add(final, back(final, parts[-1]))


def pair_scratch(tiles):
    return [
        pltpu.VMEM(((tiles + 1) * 16, TILE), jnp.float32),
        pltpu.VMEM(((tiles + 1) * 8, TILE), jnp.float32),
        *[pltpu.VMEM((64, FIELDS * TILE), jnp.bfloat16)] * UNROLL,
        *[pltpu.VMEM((TILE, FIELDS * TILE), jnp.float32)] * UNROLL,
        *[pltpu.VMEM((TILE, 6 * TILE), jnp.bfloat16)] * UNROLL,
        pltpu.VMEM((16, 6 * TILE), jnp.bfloat16),
    ]


def scan(low, high, partners, alive, chosen):
    def some(block, found):
        pairs = [block * 16 + k for k in range(16)]
        slots = [partners[p] for p in pairs]
        owners = [alive[block * 8 + k] for k in range(8)]
        others = [alive[slot] for slot in slots]
        for k in range(16):
            good = (slots[k] >= low) & (slots[k] < high) & (owners[k // 2] + others[k] == 2)
            chosen[found] = pairs[k]
            found = found + good.astype(jnp.int32)
        return found

    chosen[128] = lax.fori_loop(0, 8, some, 0)


def by_field(target, force, first, number, at=0):
    width = target.shape[0] // 6
    for c in range(6):
        rows = force[pl.ds(first * 8 + c, number, stride=8), :]
        target[c * width + at : c * width + at + number, :] = rows


def pairs_kernel(kind, listed, pushed, *refs):
    refs = list(refs)
    partners, chosen, shift, masks, start = (refs.pop(0) for _ in range(5))
    sides = [refs.pop(0) for _ in range(2)] if kind == "far" else ()
    ghosts = {"own": 0, "x": 1, "y": 2, "far": 2}[kind]
    records = [refs.pop(0) for _ in range(1 + ghosts)]
    moved = [refs.pop(0) for _ in range(1 + ghosts)] if pushed else [None] * (1 + ghosts)
    number = 0 if kind == "own" else 32 if kind == "y" else 64
    low = {"own": 0, "x": 64, "y": 128, "far": 192}[kind]
    own_force = refs.pop(0)
    outs = [refs.pop(0) for _ in range(ghosts)]
    if not listed:
        alive, chosen = chosen, refs.pop(0)
        scan(low, low + ghosts * number if ghosts else 64, partners, alive, chosen)
    table, force, *scratch = refs
    tiles = 64 + ghosts * number
    table[...] = jnp.zeros_like(table)
    load_tiles(table, 0, 64, records[0], moved[0])
    for k in range(ghosts):
        if kind == "x":
            shifts = ((shift[0], 0.0), (shift[1], 0.0))
        elif kind == "y":
            shifts = ((0.0, shift[2 + k]),)
        else:
            shifts = ((shift[0], shift[2 + k]), (shift[1], shift[2 + k]))
        load_tiles(table, 64 + k * number, number, records[1 + k], moved[1 + k], shifts)
    force[0:512] = start[...]
    if ghosts:
        force[512 : tiles * 8] = jnp.zeros((tiles * 8 - 512, TILE), jnp.float32)
    run_pairs(table, force, masks, chosen, partners, max(low - 64, 0), scratch)
    if own_force.shape[0] == 384:
        by_field(own_force, force, 0, 64)
    else:
        own_force[...] = force[0:512]
    for k in range(ghosts):
        if kind == "x":
            outs[k][...] = force[512:1024]
        elif kind == "y":
            by_field(outs[k], force, 64 + 32 * k, 32)
        else:
            for c in range(6):
                outs[k][c * 96 : c * 96 + 32, :] = sides[k][c * 32 : (c + 1) * 32, :]
            by_field(outs[k], force, 64 + 64 * k, 64, 32)


def shape(*dims):
    return jax.ShapeDtypeStruct(dims, jnp.float32)


def pairs(kind, partners, listing, shift, masks, start, records, moved=(), sides=(), last=False):
    listed = listing.shape[0] == 136
    outs = {"own": [], "x": [512], "y": [192, 192], "far": [576, 576]}[kind]
    shapes = [shape(rows, TILE) for rows in [384 if last else 512] + outs]
    places = [VMEM] * len(shapes)
    if not listed:
        shapes.append(jax.ShapeDtypeStruct((136,), jnp.int32))
        places.append(SMEM)
    return pl.pallas_call(
        functools.partial(pairs_kernel, kind, listed, bool(moved)),
        out_shape=shapes,
        in_specs=[SMEM] * 3 + [VMEM] * (2 + len(sides) + len(records) + len(moved)),
        out_specs=places,
        scratch_shapes=pair_scratch({"own": 64, "x": 128, "y": 128, "far": 192}[kind]),
        compiler_params=params(),
        cost_estimate=cost(60_000_000, 2_000_000),
        name=kind + "_pairs",
    )(partners, listing, shift, masks, start, *sides, *records, *moved)


def pack_kernel(count, position, velocity, spin, radius, exports, packed, lists, sems):
    moves = [(position, 0, 192), (velocity, 192, 192), (spin, 384, 192), (radius, 576, 64)]
    copies = [
        pltpu.make_async_copy(source, packed.at[pl.ds(first, rows)], sems.at[k])
        for k, (source, first, rows) in enumerate(moves)
    ]
    copies.append(pltpu.make_async_copy(exports, lists, sems.at[4]))
    for copy in copies:
        copy.start()
    packed[640:648] = jnp.zeros((8, TILE), jnp.float32)
    at = (64, TILE)
    index = lax.broadcasted_iota(jnp.int32, at, 0) * TILE + lax.broadcasted_iota(jnp.int32, at, 1)
    for copy in copies:
        copy.wait()
    packed[576:640] = jnp.where(index < count[0, 0], packed[576:640], DEAD)
    packed[640:648, 0:32] = lists[...].astype(jnp.float32)


def pack(count, position, velocity, spin, radius, exports):
    return pl.pallas_call(
        pack_kernel,
        out_shape=shape(648, TILE),
        in_specs=[SMEM] + [pl.BlockSpec(memory_space=pltpu.HBM)] * 5,
        out_specs=VMEM,
        scratch_shapes=[pltpu.VMEM((8, 32), jnp.int32), pltpu.SemaphoreType.DMA((5,))],
        compiler_params=pltpu.CompilerParams(vmem_limit_bytes=65_800_000),
        cost_estimate=cost(100_000, 700_000),
        name="pack",
    )(count, position, velocity, spin, radius, exports)


def copy_tile(rows, source, tile, target, place, width):
    target[pl.ds(place, rows, stride=width), :] = source[pl.ds(tile, rows, stride=64), :]


def pick_own_kernel(rows, lists, own, even, odd):
    def some(block, carry):
        for k in range(4):
            e = block * 4 + k
            copy_tile(rows, own, lists[e], even, e, 32)
            copy_tile(rows, own, lists[96 + e], odd, e, 32)
        return carry

    lax.fori_loop(0, 8, some, 0)


def pick_kernel(rows, lists, near, next_, even, odd, ghost):
    sources = (near, next_)

    def some(block, carry):
        for k in range(4):
            e = block * 4 + k
            for which in range(2):
                place = which * 32 + e
                copy_tile(rows, sources[which], lists[32 + place], even, place, 64)
                copy_tile(rows, sources[which], lists[128 + place], odd, place, 64)
                copy_tile(rows, sources[which], lists[192 + place], ghost, place, 64)
        return carry

    lax.fori_loop(0, 8, some, 0)


def pick_own(rows, lists, own):
    return pl.pallas_call(
        functools.partial(pick_own_kernel, rows),
        out_shape=(shape(rows * 32, TILE),) * 2,
        in_specs=[SMEM, VMEM],
        out_specs=(VMEM,) * 2,
        compiler_params=params(),
        cost_estimate=cost(1_000_000, 1_000_000),
        name="pick_own",
    )(lists, own)


def pick(rows, lists, near, next_):
    return pl.pallas_call(
        functools.partial(pick_kernel, rows),
        out_shape=(shape(rows * 64, TILE),) * 3,
        in_specs=[SMEM, VMEM, VMEM],
        out_specs=(VMEM,) * 3,
        compiler_params=params(),
        cost_estimate=cost(1_000_000, 3_000_000),
        name="pick",
    )(lists, near, next_)


def gather_kernel(lists, ghost, even, odd, own_total, near, next_, acc):
    acc[...] = jnp.zeros_like(acc)

    def add(tile, value):
        at = pl.ds(pl.multiple_of(tile * 8, 8), value.shape[0])
        acc[at, :] = acc[at, :] + value

    def some(block, carry):
        for k in range(4):
            e = block * 4 + k
            for which in range(3):
                add(lists[which * 32 + e] + which * 64, even[pl.ds(which * 32 + e, 6, stride=96), :])
                add(lists[96 + which * 32 + e] + which * 64, odd[pl.ds(which * 32 + e, 6, stride=96), :])
            for which in range(2):
                place = which * 32 + e
                value = ghost[pl.ds(pl.multiple_of(place * 8, 8), 8), :]
                add(lists[192 + place] + (1 + which) * 64, value)
        return carry

    lax.fori_loop(0, 8, some, 0)
    for k, total in enumerate((own_total, near, next_)):
        by_field(total, acc, 64 * k, 64)


def gather(lists, ghost, even, odd):
    return pl.pallas_call(
        gather_kernel,
        out_shape=(shape(384, TILE),) * 3,
        in_specs=[SMEM, VMEM, VMEM, VMEM],
        out_specs=(VMEM,) * 3,
        scratch_shapes=[pltpu.VMEM((1536, TILE), jnp.float32)],
        compiler_params=params(),
        cost_estimate=cost(1_000_000, 3_000_000),
        name="gather",
    )(lists, ghost, even, odd)


def local(positions, velocities, spins, radii, counts, exports, partners, masks):
    tiles = radii.shape[-1] // TILE
    count = counts[0, 0]
    chosen = exports[0, 0]
    words = masks[0, 0]
    packed = pack(
        counts,
        positions.reshape(3 * tiles, TILE),
        velocities.reshape(3 * tiles, TILE),
        spins.reshape(3 * tiles, TILE),
        radii.reshape(tiles, TILE),
        chosen,
    )
    got_y = swap(packed, "gx", 1)
    got_x = swap(packed, "gx", 0)
    state = packed
    position, velocity, spin = (packed[k * tiles : (k + 3) * tiles].reshape(3, tiles, TILE) for k in (0, 3, 6))
    radius = packed[9 * tiles : 10 * tiles].reshape(1, tiles, TILE)
    live = (radius > 0.0).astype(jnp.float32)
    mass = mass_scale * radius * radius * radius
    inertia = 0.4 * mass * radius * radius
    lift = jnp.array([0.0, 0.0, -gravity], jnp.float32)[:, None, None]

    odd_x = lax.rem(lax.axis_index("gx"), 2)
    odd_y = lax.rem(lax.axis_index("gy"), 2)
    east = {0: odd_x == 1, 1: odd_x == 0}
    north = {0: odd_y == 0, 1: odd_y == 1}

    def choose(table, which):
        return lax.dynamic_index_in_dim(table, which, 0, keepdims=False)

    def face(a):
        return jnp.where(a, 0, 1)

    def side(b):
        return jnp.where(b, 2, 3)

    def corner(a, b):
        return jnp.where(a, jnp.where(b, 4, 5), jnp.where(b, 6, 7))

    west_at = jnp.where(odd_x == 1, 0, 1)
    south_at = jnp.where(odd_y == 1, 0, 1)
    x_of = (west_at, 1 - west_at)
    y_of = (south_at, 1 - south_at)
    block_of = [
        x_of[0],
        x_of[1],
        2 + y_of[0],
        2 + y_of[1],
        4 + 2 * y_of[0] + x_of[0],
        4 + 2 * y_of[1] + x_of[0],
        4 + 2 * y_of[0] + x_of[1],
        4 + 2 * y_of[1] + x_of[1],
    ]
    block_of = jnp.stack(block_of).astype(jnp.int32)
    listed = partners[0, 0]
    kind = jnp.maximum(listed - tiles, 0) // 32
    hot = (kind[:, None] == jnp.arange(8, dtype=jnp.int32)[None, :]).astype(jnp.int32)
    slots = jnp.where(
        listed < tiles,
        listed,
        tiles + 32 * jnp.sum(hot * block_of[None, :], axis=1) + lax.rem(jnp.maximum(listed - tiles, 0), 32),
    )
    own_alive = (jnp.arange(tiles, dtype=jnp.int32) * TILE < count).astype(jnp.int32)

    shift = jnp.stack(
        [
            jnp.where(east[0], -column_width, column_width),
            jnp.where(east[1], -column_width, column_width),
            jnp.where(north[0], column_width, -column_width),
            jnp.where(north[1], column_width, -column_width),
        ]
    ).astype(jnp.float32)
    nothing = jnp.zeros((tiles * 8, TILE), jnp.float32)

    def alive_in(record):
        return (record[9 * record.shape[0] // 10 :, 0] > 0.0).astype(jnp.int32)

    def exchange_sides(rows, lists, own):
        to_even, to_odd = pick_own(rows, lists, own)
        return swap(to_even, "gy", 0), swap(to_odd, "gy", 1)

    own_lists = [choose(chosen, side(north[0])), choose(chosen, side(north[1]))]

    for step in range(STEPS):
        if step == 0:
            blank = jnp.zeros((64,), jnp.int32)
            lists = jnp.concatenate([own_lists[0], blank, own_lists[1], blank, blank])
            even_side, odd_side = exchange_sides(10, lists, state)
            list_x = got_x[10 * tiles :, 0:32].astype(jnp.int32)
            list_y = got_y[10 * tiles :, 0:32].astype(jnp.int32)
            lists = jnp.stack(
                [
                    own_lists[0],
                    choose(list_x, corner(east[0], north[0])),
                    choose(list_y, corner(east[1], north[0])),
                    own_lists[1],
                    choose(list_x, corner(east[0], north[1])),
                    choose(list_y, corner(east[1], north[1])),
                    choose(list_x, face(east[0])),
                    choose(list_y, face(east[1])),
                ]
            ).reshape(256)
            to_even, to_odd, ghost = pick(10, lists, got_x, got_y)
            even, odd = swap(to_even, "gy", 0), swap(to_odd, "gy", 1)
            alive = jnp.concatenate([own_alive, alive_in(ghost), alive_in(even_side), alive_in(odd_side)])
            near_alive = jnp.concatenate([alive, jnp.zeros((128,), jnp.int32)])
            own_force, *sides, y_list = pairs(
                "y", slots, near_alive, shift, words, nothing, (state, even_side, odd_side)
            )
            even, odd, own_force = lax.optimization_barrier((even, odd, own_force))
            far_alive = jnp.concatenate([alive, alive_in(even), alive_in(odd)])
            own_force, even_force, odd_force, far_list = pairs(
                "far", slots, far_alive, shift, words, own_force, (state, even, odd), (), sides
            )
            back_odd, back_even = swap(odd_force, "gy", 1), swap(even_force, "gy", 0)
            own_force, ghost_force, x_list = pairs("x", slots, near_alive, shift, words, own_force, (state, ghost))
        else:
            new = jnp.concatenate([velocity, spin], axis=0).reshape(6 * tiles, TILE)
            got_y = swap(new, "gx", 1)
            got_x = swap(new, "gx", 0)
            to_even, to_odd = pick_own(6, lists, new)
            even_side_new, odd_side_new = swap(to_even, "gy", 0), swap(to_odd, "gy", 1)
            got_x, got_y, even_side_new, odd_side_new = lax.optimization_barrier(
                (got_x, got_y, even_side_new, odd_side_new)
            )
            to_even, to_odd, ghost_new = pick(6, lists, got_x, got_y)
            even_new, odd_new = swap(to_even, "gy", 0), swap(to_odd, "gy", 1)
            early, _ = lax.optimization_barrier((nothing, to_even))
            own_force, *sides = pairs(
                "y",
                slots,
                y_list,
                shift,
                words,
                early,
                (state, even_side, odd_side),
                (new, even_side_new, odd_side_new),
            )
            even_new, odd_new, own_force = lax.optimization_barrier((even_new, odd_new, own_force))
            own_force, even_force, odd_force = pairs(
                "far", slots, far_list, shift, words, own_force, (state, even, odd), (new, even_new, odd_new), sides
            )
            back_odd, back_even = swap(odd_force, "gy", 1), swap(even_force, "gy", 0)
            own_force, ghost_force = pairs(
                "x", slots, x_list, shift, words, own_force, (state, ghost), (new, ghost_new)
            )
        back_odd, back_even, own_force = lax.optimization_barrier((back_odd, back_even, own_force))
        own_total, to_x, to_y = gather(lists, ghost_force, back_even, back_odd)
        back_y = swap(to_y, "gx", 1)
        back_x = swap(to_x, "gx", 0)
        own_total, own_force = lax.optimization_barrier((own_total, own_force))
        if step == 0:
            last_force, own_list = pairs("own", slots, near_alive, shift, words, own_force, (state,), last=True)
        else:
            (last_force,) = pairs(
                "own",
                slots,
                own_list,
                shift,
                words,
                own_force,
                (state,),
                (new,),
                last=True,
            )
        force = sum(part.reshape(6, tiles, TILE) for part in (own_total, back_x, back_y, last_force))
        velocity = velocity + time_step * live * (force[0:3] / mass + lift)
        spin = spin + time_step * live * force[3:6] / inertia
        position = position + time_step * live * velocity
    result = (1, 1, 3, tiles * TILE)
    return (position.reshape(result), velocity.reshape(result), spin.reshape(result))


def solution(mesh):
    return jax.shard_map(
        local,
        mesh=mesh,
        in_specs=(
            P("gx", "gy", None, None),
            P("gx", "gy", None, None),
            P("gx", "gy", None, None),
            P("gx", "gy", None),
            P("gx", "gy"),
            P("gx", "gy", None, None),
            P("gx", "gy", None),
            P("gx", "gy", None, None, None),
        ),
        out_specs=(P("gx", "gy", None, None), P("gx", "gy", None, None), P("gx", "gy", None, None)),
        check_vma=False,
    )
```

```python
import functools

import jax
import jax.numpy as jnp
from jax import lax
from jax.experimental import pallas as pl
from jax.experimental.pallas import tpu as pltpu
from jax.sharding import PartitionSpec as P

TILE = 128
STEPS = 2
SECOND_PARTS = ((0, 5, 12), (5, 12, 12))
BLOCK = 32
UNROLL = 2

stiffness = 1.0
damping_normal = 0.5
damping_tangent = 0.3
softening = 0.05
time_step = 0.25
column_width = 3.0
gravity = 1.0
mass_scale = 8.0

DEAD = -10.0

VMEM = pl.BlockSpec(memory_space=pltpu.VMEM)
SMEM = pl.BlockSpec(memory_space=pltpu.SMEM)
VMEM_LIMIT = 20 * 1024 * 1024


def swap(value, axis, odd):
    count = lax.axis_size(axis)
    pairs = []
    for i in range(odd, count, 2):
        k = (i + 1) % count
        pairs += [(i, k), (k, i)]
    return lax.ppermute(value, axis, pairs)


def params():
    return pltpu.CompilerParams(vmem_limit_bytes=VMEM_LIMIT)


def cost(flops, size):
    return pl.CostEstimate(flops=flops, bytes_accessed=size, transcendentals=0)


def cross(a, b):
    return (
        a[1] * b[2] - a[2] * b[1],
        a[2] * b[0] - a[0] * b[2],
        a[0] * b[1] - a[1] * b[0],
    )


FIELDS = 10


def split(value):
    high = value.astype(jnp.bfloat16).astype(jnp.float32)
    rest = value - high
    middle = rest.astype(jnp.bfloat16).astype(jnp.float32)
    return high, middle, rest - middle


def fill_constants(spread, sums):
    sub = lax.broadcasted_iota(jnp.int32, (64, TILE), 0)
    for c in range(FIELDS):
        here = (lax.rem(sub, 16) == c) & (sub < 48)
        for ref in spread:
            ref[:, c * TILE : (c + 1) * TILE] = here.astype(jnp.float32).astype(jnp.bfloat16)
    row = lax.broadcasted_iota(jnp.int32, (16, 6 * TILE), 0)
    column = lax.rem(lax.broadcasted_iota(jnp.int32, (16, 6 * TILE), 1) // (TILE // 2), 6)
    sums[...] = (row == column).astype(jnp.float32).astype(jnp.bfloat16)


def combine(rec_i, rec_j, spread, both):
    high, middle, low = split(rec_i)
    sub = lax.broadcasted_iota(jnp.int32, (16, TILE), 0)
    for c in range(10):
        rows = jnp.where(
            sub == 0,
            high[c : c + 1],
            jnp.where(sub == 1, middle[c : c + 1], jnp.where(sub == 2, low[c : c + 1], 0.0)),
        )
        if c < 6:
            rows = -rows
        spread[48:64, c * TILE : (c + 1) * TILE] = rows.astype(jnp.bfloat16)
    high, middle, low = split(rec_j)
    left = jnp.concatenate(
        [high, middle, low, jnp.ones((16, TILE), jnp.float32), jnp.zeros((64, TILE), jnp.float32)], axis=0
    )
    left = jnp.transpose(left)[:, 0:64].astype(jnp.bfloat16)
    both[...] = jnp.dot(left, spread[...], preferred_element_type=jnp.float32)


def fold(first, second):
    low = lax.broadcasted_iota(jnp.int32, first.shape, 1) < TILE // 2
    kept = jnp.where(low, first, second)
    other = jnp.where(low, second, first)
    return kept + pltpu.roll(other, TILE // 2, 1)


def pair_forces(rec_i, words, both, parts):
    radius_i = rec_i[9:10, :]
    scaled = damping_tangent * damping_tangent * radius_i
    sub = lax.broadcasted_iota(jnp.int32, (8, TILE), 0)
    bit = jnp.left_shift(1, sub)
    sums_i = [jnp.zeros((8, TILE), jnp.float32) for _ in range(6)]
    for first in range(0, TILE, BLOCK):
        field = [both[first : first + BLOCK, c * TILE : (c + 1) * TILE] for c in range(FIELDS)]
        r, dv, spin = field[0:3], field[3:6], field[6:9]
        d2 = r[0] * r[0] + r[1] * r[1] + (r[2] * r[2] + softening * softening)
        inv = lax.rsqrt(d2)
        inter = jnp.maximum(field[9] - d2 * inv, 0.0)
        top = (field[9] - radius_i) * scaled * inter
        root = top * lax.rsqrt(jnp.maximum(top * field[9], 1e-30))
        hit = jnp.concatenate(
            [
                (jnp.broadcast_to(words[w : w + 1, :], (8, TILE)) & bit) != 0
                for w in range(first // 8, (first + BLOCK) // 8)
            ],
            axis=0,
        )
        k2 = jnp.where(hit, root, 0.0)
        n = [inv * x for x in r]
        speed_n = dv[0] * n[0] + dv[1] * n[1] + dv[2] * n[2]
        k1 = k2 * (
            (stiffness / damping_tangent) * inter
            - ((damping_normal - damping_tangent) / damping_tangent) * speed_n
        )
        turn = cross(spin, n)
        drag = [k2 * (dv[c] - turn[c]) for c in range(3)]
        terms = [drag[c] - k1 * n[c] for c in range(3)] + list(cross(n, drag))
        for c in range(6):
            part = terms[c]
            sums_i[c] = sums_i[c] + sum(part[8 * q : 8 * q + 8] for q in range(BLOCK // 8))
        for c in range(3):
            part = fold(terms[2 * c], terms[2 * c + 1])
            high = part.astype(jnp.bfloat16)
            low = (part - high.astype(jnp.float32)).astype(jnp.bfloat16)
            parts[first : first + BLOCK, c * TILE : (c + 1) * TILE] = high
            parts[first : first + BLOCK, (3 + c) * TILE : (4 + c) * TILE] = low
    own = jnp.zeros((8, TILE), jnp.float32)
    for c in range(6):
        own = jnp.where(sub == c, jnp.sum(sums_i[c], axis=0, keepdims=True), own)
    own = own * jnp.where(sub < 3, 1.0, radius_i)
    return own


def forces_back(rec_j, parts, sums):
    over = (((1,), (1,)), ((), ()))
    back = lax.dot_general(sums[...], parts[...], over, preferred_element_type=jnp.float32)
    sub = lax.broadcasted_iota(jnp.int32, (8, TILE), 0)
    return back[0:8] * jnp.where(sub < 3, -1.0, rec_j[9:10, :])


def load_tiles(table, first, number, record, moved=None, shifts=()):
    def rows(ref, c):
        return ref[c * number : (c + 1) * number, :]

    radius = rows(record, 9)
    live = jnp.where(radius > 0.0, 1.0, 0.0)
    for c in range(10):
        if c == 9:
            value = radius
        elif moved is None:
            value = rows(record, c)
        elif c < 3:
            value = rows(record, c) + time_step * live * rows(moved, c)
        else:
            value = rows(moved, c - 3)
        if 6 <= c < 9:
            value = value * radius
        if c < 2 and shifts:
            value = jnp.concatenate([value[32 * k : 32 * k + 32] + at[c] for k, at in enumerate(shifts)], axis=0)
        table[pl.ds(first * 16 + c, number, stride=16), :] = value


def run_pairs(table, force, masks, chosen, partners, skipped, scratch, part):
    spread, both, parts = (scratch[k * UNROLL : (k + 1) * UNROLL] for k in range(3))
    sums = scratch[3 * UNROLL]
    fill_constants(spread, sums)
    last = force.shape[0] // 8 - 1
    table[last * 16 : last * 16 + 16] = jnp.full((16, TILE), DEAD, jnp.float32)
    force[last * 8 : last * 8 + 8] = jnp.zeros((8, TILE), jnp.float32)

    found = chosen[128]
    origin, number = found * part[0] // part[2], found * part[1] // part[2]

    def entry(n):
        real = n + origin < number
        p = jnp.where(real, chosen[jnp.minimum(n + origin, 127)], 0)
        owner = jnp.where(real, p // 2, last)
        place = jnp.where(real, partners[p] - skipped, last)
        return p, owner, place

    def record(tile):
        return table[pl.ds(pl.multiple_of(tile * 16, 16), 16), :]

    def prepare(item, spread, both):
        combine(record(item[1]), record(item[2]), spread, both)

    def forces(item, both, parts):
        return pair_forces(record(item[1]), masks[item[0]], both, parts)

    def back(place, parts):
        return forces_back(record(place), parts, sums)

    def add(tile, value):
        at = pl.ds(pl.multiple_of(tile * 8, 8), 8)
        force[at, :] = force[at, :] + value

    parts[-1][...] = jnp.zeros_like(parts[-1])
    prepare(entry(0), spread[0], both[0])

    def some(t, before):
        items = [entry(UNROLL * t + k) for k in range(UNROLL + 1)]
        results = []
        place = before
        for k in range(UNROLL):
            after = (k + 1) % UNROLL
            prepare(items[k + 1], spread[after], both[after])
            results.append((place, back(place, parts[k - 1])))
            results.append((items[k][1], forces(items[k], both[k], parts[k])))
            place = items[k][2]
        for tile, value in results:
            add(tile, value)
        return place

    final = lax.fori_loop(0, (number - origin + UNROLL - 1) // UNROLL, some, jnp.int32(last))
    add(final, back(final, parts[-1]))


def pair_scratch(tiles):
    return [
        pltpu.VMEM(((tiles + 1) * 16, TILE), jnp.float32),
        pltpu.VMEM(((tiles + 1) * 8, TILE), jnp.float32),
        *[pltpu.VMEM((64, FIELDS * TILE), jnp.bfloat16)] * UNROLL,
        *[pltpu.VMEM((TILE, FIELDS * TILE), jnp.float32)] * UNROLL,
        *[pltpu.VMEM((TILE, 6 * TILE), jnp.bfloat16)] * UNROLL,
        pltpu.VMEM((16, 6 * TILE), jnp.bfloat16),
    ]


def scan(low, high, partners, alive, chosen):
    def some(block, found):
        pairs = [block * 16 + k for k in range(16)]
        slots = [partners[p] for p in pairs]
        owners = [alive[block * 8 + k] for k in range(8)]
        others = [alive[slot] for slot in slots]
        for k in range(16):
            good = (slots[k] >= low) & (slots[k] < high) & (owners[k // 2] + others[k] == 2)
            chosen[found] = pairs[k]
            found = found + good.astype(jnp.int32)
        return found

    chosen[128] = lax.fori_loop(0, 8, some, 0)


def by_field(target, force, number):
    for c in range(6):
        target[c * number : (c + 1) * number, :] = force[pl.ds(c, number, stride=8), :]


def by_tile(target, at, force, first, number):
    for k in range(number):
        target[(at + k) * 6 : (at + k) * 6 + 6, :] = force[(first + k) * 8 : (first + k) * 8 + 6, :]


def pairs_kernel(kind, part, listed, pushed, *refs):
    refs = list(refs)
    partners, chosen, shift, masks, start = (refs.pop(0) for _ in range(5))
    sides = [refs.pop(0) for _ in range(2)] if kind == "far" else ()
    ghosts = {"own": 0, "x": 1, "y": 2, "far": 2}[kind]
    records = [refs.pop(0) for _ in range(1 + ghosts)]
    moved = [refs.pop(0) for _ in range(1 + ghosts)] if pushed else [None] * (1 + ghosts)
    number = 0 if kind == "own" else 32 if kind == "y" else 64
    low = {"own": 0, "x": 64, "y": 128, "far": 192}[kind]
    own_force = refs.pop(0)
    outs = [refs.pop(0) for _ in range(ghosts)]
    if not listed:
        alive, chosen = chosen, refs.pop(0)
        scan(low, low + ghosts * number if ghosts else 64, partners, alive, chosen)
    table, force, *scratch = refs
    tiles = 64 + ghosts * number
    table[...] = jnp.zeros_like(table)
    load_tiles(table, 0, 64, records[0], moved[0])
    for k in range(ghosts):
        if kind == "x":
            shifts = ((shift[0], 0.0), (shift[1], 0.0))
        elif kind == "y":
            shifts = ((0.0, shift[2 + k]),)
        else:
            shifts = ((shift[0], shift[2 + k]), (shift[1], shift[2 + k]))
        load_tiles(table, 64 + k * number, number, records[1 + k], moved[1 + k], shifts)
    force[0:512] = start[...]
    if ghosts:
        force[512 : tiles * 8] = jnp.zeros((tiles * 8 - 512, TILE), jnp.float32)
    run_pairs(table, force, masks, chosen, partners, max(low - 64, 0), scratch, part)
    if own_force.shape[0] == 384:
        by_field(own_force, force, 64)
    else:
        own_force[...] = force[0:512]
    for k in range(ghosts):
        if kind == "x":
            outs[k][...] = force[512:1024]
        elif kind == "y":
            by_tile(outs[k], 0, force, 64 + 32 * k, 32)
        else:
            outs[k][0:192] = sides[k][...]
            by_tile(outs[k], 32, force, 64 + 64 * k, 64)


def shape(*dims):
    return jax.ShapeDtypeStruct(dims, jnp.float32)


def pairs(kind, partners, listing, shift, masks, start, records, moved=(), sides=(), part=(0, 1, 1), last=False):
    listed = listing.shape[0] == 136
    outs = {"own": [], "x": [512], "y": [192, 192], "far": [576, 576]}[kind]
    shapes = [shape(rows, TILE) for rows in [384 if last else 512] + outs]
    places = [VMEM] * len(shapes)
    if not listed:
        shapes.append(jax.ShapeDtypeStruct((136,), jnp.int32))
        places.append(SMEM)
    return pl.pallas_call(
        functools.partial(pairs_kernel, kind, part, listed, bool(moved)),
        out_shape=shapes,
        in_specs=[SMEM] * 3 + [VMEM] * (2 + len(sides) + len(records) + len(moved)),
        out_specs=places,
        scratch_shapes=pair_scratch({"own": 64, "x": 128, "y": 128, "far": 192}[kind]),
        compiler_params=params(),
        cost_estimate=cost(60_000_000, 2_000_000),
        name=kind + "_pairs",
    )(partners, listing, shift, masks, start, *sides, *records, *moved)


def pack_kernel(count, position, velocity, spin, radius, exports, packed, lists, sems):
    moves = [(position, 0, 192), (velocity, 192, 192), (spin, 384, 192), (radius, 576, 64)]
    copies = [
        pltpu.make_async_copy(source, packed.at[pl.ds(first, rows)], sems.at[k])
        for k, (source, first, rows) in enumerate(moves)
    ]
    copies.append(pltpu.make_async_copy(exports, lists, sems.at[4]))
    for copy in copies:
        copy.start()
    packed[640:648] = jnp.zeros((8, TILE), jnp.float32)
    at = (64, TILE)
    index = lax.broadcasted_iota(jnp.int32, at, 0) * TILE + lax.broadcasted_iota(jnp.int32, at, 1)
    for copy in copies:
        copy.wait()
    packed[576:640] = jnp.where(index < count[0, 0], packed[576:640], DEAD)
    packed[640:648, 0:32] = lists[...].astype(jnp.float32)


def pack(count, position, velocity, spin, radius, exports):
    return pl.pallas_call(
        pack_kernel,
        out_shape=shape(648, TILE),
        in_specs=[SMEM] + [pl.BlockSpec(memory_space=pltpu.HBM)] * 5,
        out_specs=VMEM,
        scratch_shapes=[pltpu.VMEM((8, 32), jnp.int32), pltpu.SemaphoreType.DMA((5,))],
        compiler_params=pltpu.CompilerParams(vmem_limit_bytes=65_800_000),
        cost_estimate=cost(100_000, 700_000),
        name="pack",
    )(count, position, velocity, spin, radius, exports)


def copy_tile(rows, source, tile, target, place, width):
    target[pl.ds(place, rows, stride=width), :] = source[pl.ds(tile, rows, stride=64), :]


def pick_own_kernel(rows, lists, own, even, odd):
    def some(block, carry):
        for k in range(4):
            e = block * 4 + k
            copy_tile(rows, own, lists[e], even, e, 32)
            copy_tile(rows, own, lists[96 + e], odd, e, 32)
        return carry

    lax.fori_loop(0, 8, some, 0)


def pick_kernel(rows, lists, near, next_, even, odd, ghost):
    sources = (near, next_)

    def some(block, carry):
        for k in range(4):
            e = block * 4 + k
            for which in range(2):
                place = which * 32 + e
                copy_tile(rows, sources[which], lists[32 + place], even, place, 64)
                copy_tile(rows, sources[which], lists[128 + place], odd, place, 64)
                copy_tile(rows, sources[which], lists[192 + place], ghost, place, 64)
        return carry

    lax.fori_loop(0, 8, some, 0)


def pick_own(rows, lists, own):
    return pl.pallas_call(
        functools.partial(pick_own_kernel, rows),
        out_shape=(shape(rows * 32, TILE),) * 2,
        in_specs=[SMEM, VMEM],
        out_specs=(VMEM,) * 2,
        compiler_params=params(),
        cost_estimate=cost(1_000_000, 1_000_000),
        name="pick_own",
    )(lists, own)


def pick(rows, lists, near, next_):
    return pl.pallas_call(
        functools.partial(pick_kernel, rows),
        out_shape=(shape(rows * 64, TILE),) * 3,
        in_specs=[SMEM, VMEM, VMEM],
        out_specs=(VMEM,) * 3,
        compiler_params=params(),
        cost_estimate=cost(1_000_000, 3_000_000),
        name="pick",
    )(lists, near, next_)


def gather_kernel(lists, ghost, even, odd, own_total, near, next_, *sums):
    for ref in sums:
        ref[...] = jnp.zeros_like(ref)

    def add(ref, tile, value):
        at = pl.ds(pl.multiple_of(tile * 8, 8), value.shape[0])
        ref[at, :] = ref[at, :] + value

    def some(block, carry):
        for k in range(4):
            e = block * 4 + k
            for which in range(3):
                place = which * 32 + e
                add(sums[which], lists[place], even[pl.ds(place * 6, 6), :])
                add(sums[3 + which], lists[96 + place], odd[pl.ds(place * 6, 6), :])
            for which in range(2):
                place = which * 32 + e
                value = ghost[pl.ds(pl.multiple_of(place * 8, 8), 8), :]
                add(sums[6 + which], lists[192 + place], value)
        return carry

    lax.fori_loop(0, 8, some, 0)
    for c in range(6):
        part = [ref[pl.ds(c, 64, stride=8), :] for ref in sums]
        own_total[c * 64 : (c + 1) * 64, :] = part[0] + part[3]
        near[c * 64 : (c + 1) * 64, :] = part[1] + part[4] + part[6]
        next_[c * 64 : (c + 1) * 64, :] = part[2] + part[5] + part[7]


def gather(lists, ghost, even, odd):
    return pl.pallas_call(
        gather_kernel,
        out_shape=(shape(384, TILE),) * 3,
        in_specs=[SMEM, VMEM, VMEM, VMEM],
        out_specs=(VMEM,) * 3,
        scratch_shapes=[pltpu.VMEM((512, TILE), jnp.float32)] * 8,
        compiler_params=params(),
        cost_estimate=cost(1_000_000, 3_000_000),
        name="gather",
    )(lists, ghost, even, odd)


def local(positions, velocities, spins, radii, counts, exports, partners, masks):
    tiles = radii.shape[-1] // TILE
    count = counts[0, 0]
    chosen = exports[0, 0]
    words = masks[0, 0]
    packed = pack(
        counts,
        positions.reshape(3 * tiles, TILE),
        velocities.reshape(3 * tiles, TILE),
        spins.reshape(3 * tiles, TILE),
        radii.reshape(tiles, TILE),
        chosen,
    )
    got_y = swap(packed, "gx", 1)
    got_x = swap(packed, "gx", 0)
    state = packed
    position, velocity, spin = (packed[k * tiles : (k + 3) * tiles].reshape(3, tiles, TILE) for k in (0, 3, 6))
    radius = packed[9 * tiles : 10 * tiles].reshape(1, tiles, TILE)
    live = (radius > 0.0).astype(jnp.float32)
    mass = mass_scale * radius * radius * radius
    inertia = 0.4 * mass * radius * radius
    lift = jnp.array([0.0, 0.0, -gravity], jnp.float32)[:, None, None]

    odd_x = lax.rem(lax.axis_index("gx"), 2)
    odd_y = lax.rem(lax.axis_index("gy"), 2)
    east = {0: odd_x == 1, 1: odd_x == 0}
    north = {0: odd_y == 0, 1: odd_y == 1}

    def choose(table, which):
        return lax.dynamic_index_in_dim(table, which, 0, keepdims=False)

    def face(a):
        return jnp.where(a, 0, 1)

    def side(b):
        return jnp.where(b, 2, 3)

    def corner(a, b):
        return jnp.where(a, jnp.where(b, 4, 5), jnp.where(b, 6, 7))

    west_at = jnp.where(odd_x == 1, 0, 1)
    south_at = jnp.where(odd_y == 1, 0, 1)
    x_of = (west_at, 1 - west_at)
    y_of = (south_at, 1 - south_at)
    block_of = [
        x_of[0],
        x_of[1],
        2 + y_of[0],
        2 + y_of[1],
        4 + 2 * y_of[0] + x_of[0],
        4 + 2 * y_of[1] + x_of[0],
        4 + 2 * y_of[0] + x_of[1],
        4 + 2 * y_of[1] + x_of[1],
    ]
    block_of = jnp.stack(block_of).astype(jnp.int32)
    listed = partners[0, 0]
    kind = jnp.maximum(listed - tiles, 0) // 32
    hot = (kind[:, None] == jnp.arange(8, dtype=jnp.int32)[None, :]).astype(jnp.int32)
    slots = jnp.where(
        listed < tiles,
        listed,
        tiles + 32 * jnp.sum(hot * block_of[None, :], axis=1) + lax.rem(jnp.maximum(listed - tiles, 0), 32),
    )
    own_alive = (jnp.arange(tiles, dtype=jnp.int32) * TILE < count).astype(jnp.int32)

    shift = jnp.stack(
        [
            jnp.where(east[0], -column_width, column_width),
            jnp.where(east[1], -column_width, column_width),
            jnp.where(north[0], column_width, -column_width),
            jnp.where(north[1], column_width, -column_width),
        ]
    ).astype(jnp.float32)
    nothing = jnp.zeros((tiles * 8, TILE), jnp.float32)

    def alive_in(record):
        return (record[9 * record.shape[0] // 10 :, 0] > 0.0).astype(jnp.int32)

    def exchange_sides(rows, lists, own):
        to_even, to_odd = pick_own(rows, lists, own)
        return swap(to_even, "gy", 0), swap(to_odd, "gy", 1)

    own_lists = [choose(chosen, side(north[0])), choose(chosen, side(north[1]))]

    for step in range(STEPS):
        if step == 0:
            blank = jnp.zeros((64,), jnp.int32)
            lists = jnp.concatenate([own_lists[0], blank, own_lists[1], blank, blank])
            even_side, odd_side = exchange_sides(10, lists, state)
            list_x = got_x[10 * tiles :, 0:32].astype(jnp.int32)
            list_y = got_y[10 * tiles :, 0:32].astype(jnp.int32)
            lists = jnp.stack(
                [
                    own_lists[0],
                    choose(list_x, corner(east[0], north[0])),
                    choose(list_y, corner(east[1], north[0])),
                    own_lists[1],
                    choose(list_x, corner(east[0], north[1])),
                    choose(list_y, corner(east[1], north[1])),
                    choose(list_x, face(east[0])),
                    choose(list_y, face(east[1])),
                ]
            ).reshape(256)
            to_even, to_odd, ghost = pick(10, lists, got_x, got_y)
            even, odd = swap(to_even, "gy", 0), swap(to_odd, "gy", 1)
            alive = jnp.concatenate([own_alive, alive_in(ghost), alive_in(even_side), alive_in(odd_side)])
            near_alive = jnp.concatenate([alive, jnp.zeros((128,), jnp.int32)])
            own_force, *sides, y_list = pairs(
                "y", slots, near_alive, shift, words, nothing, (state, even_side, odd_side)
            )
            even, odd, own_force = lax.optimization_barrier((even, odd, own_force))
            far_alive = jnp.concatenate([alive, alive_in(even), alive_in(odd)])
            own_force, even_force, odd_force, far_list = pairs(
                "far", slots, far_alive, shift, words, own_force, (state, even, odd), (), sides
            )
            back_odd, back_even = swap(odd_force, "gy", 1), swap(even_force, "gy", 0)
            own_force, ghost_force, x_list = pairs("x", slots, near_alive, shift, words, own_force, (state, ghost))
        else:
            new = jnp.concatenate([velocity, spin], axis=0).reshape(6 * tiles, TILE)
            got_y = swap(new, "gx", 1)
            got_x = swap(new, "gx", 0)
            to_even, to_odd = pick_own(6, lists, new)
            even_side_new, odd_side_new = swap(to_even, "gy", 0), swap(to_odd, "gy", 1)
            early, _ = lax.optimization_barrier((nothing, to_even))
            own_force = pairs(
                "own", slots, own_list, shift, words, early, (state,), (new,), part=SECOND_PARTS[0]
            )[0]
            got_x, got_y, even_side_new, odd_side_new, own_force = lax.optimization_barrier(
                (got_x, got_y, even_side_new, odd_side_new, own_force)
            )
            to_even, to_odd, ghost_new = pick(6, lists, got_x, got_y)
            even_new, odd_new = swap(to_even, "gy", 0), swap(to_odd, "gy", 1)
            own_force, _ = lax.optimization_barrier((own_force, to_even))
            own_force, *sides = pairs(
                "y",
                slots,
                y_list,
                shift,
                words,
                own_force,
                (state, even_side, odd_side),
                (new, even_side_new, odd_side_new),
            )
            even_new, odd_new, own_force = lax.optimization_barrier((even_new, odd_new, own_force))
            own_force, even_force, odd_force = pairs(
                "far", slots, far_list, shift, words, own_force, (state, even, odd), (new, even_new, odd_new), sides
            )
            back_odd, back_even = swap(odd_force, "gy", 1), swap(even_force, "gy", 0)
            own_force, ghost_force = pairs(
                "x", slots, x_list, shift, words, own_force, (state, ghost), (new, ghost_new)
            )
        back_odd, back_even, own_force = lax.optimization_barrier((back_odd, back_even, own_force))
        own_total, to_x, to_y = gather(lists, ghost_force, back_even, back_odd)
        back_y = swap(to_y, "gx", 1)
        back_x = swap(to_x, "gx", 0)
        own_total, own_force = lax.optimization_barrier((own_total, own_force))
        if step == 0:
            last_force, own_list = pairs("own", slots, near_alive, shift, words, own_force, (state,), last=True)
        else:
            (last_force,) = pairs(
                "own",
                slots,
                own_list,
                shift,
                words,
                own_force,
                (state,),
                (new,),
                part=SECOND_PARTS[1],
                last=True,
            )
        force = sum(part.reshape(6, tiles, TILE) for part in (own_total, back_x, back_y, last_force))
        velocity = velocity + time_step * live * (force[0:3] / mass + lift)
        spin = spin + time_step * live * force[3:6] / inertia
        position = position + time_step * live * velocity
    result = (1, 1, 3, tiles * TILE)
    return (position.reshape(result), velocity.reshape(result), spin.reshape(result))


def solution(mesh):
    return jax.shard_map(
        local,
        mesh=mesh,
        in_specs=(
            P("gx", "gy", None, None),
            P("gx", "gy", None, None),
            P("gx", "gy", None, None),
            P("gx", "gy", None),
            P("gx", "gy"),
            P("gx", "gy", None, None),
            P("gx", "gy", None),
            P("gx", "gy", None, None, None),
        ),
        out_specs=(P("gx", "gy", None, None), P("gx", "gy", None, None), P("gx", "gy", None, None)),
        check_vma=False,
    )
```

```python
import functools

import jax
import jax.numpy as jnp
from jax import lax
from jax.experimental import pallas as pl
from jax.experimental.pallas import tpu as pltpu
from jax.sharding import PartitionSpec as P

TILE = 128
STEPS = 2
SECOND_PARTS = ((0, 5, 12), (5, 12, 12))
BLOCK = 32
UNROLL = 2

stiffness = 1.0
damping_normal = 0.5
damping_tangent = 0.3
softening = 0.05
time_step = 0.25
column_width = 3.0
gravity = 1.0
mass_scale = 8.0

DEAD = -10.0

VMEM = pl.BlockSpec(memory_space=pltpu.VMEM)
SMEM = pl.BlockSpec(memory_space=pltpu.SMEM)
VMEM_LIMIT = 20 * 1024 * 1024


def swap(value, axis, odd):
    count = lax.axis_size(axis)
    pairs = []
    for i in range(odd, count, 2):
        k = (i + 1) % count
        pairs += [(i, k), (k, i)]
    return lax.ppermute(value, axis, pairs)


def params():
    return pltpu.CompilerParams(vmem_limit_bytes=VMEM_LIMIT)


def cost(flops, size):
    return pl.CostEstimate(flops=flops, bytes_accessed=size, transcendentals=0)


def cross(a, b):
    return (
        a[1] * b[2] - a[2] * b[1],
        a[2] * b[0] - a[0] * b[2],
        a[0] * b[1] - a[1] * b[0],
    )


FIELDS = 10


def split(value):
    high = value.astype(jnp.bfloat16).astype(jnp.float32)
    rest = value - high
    middle = rest.astype(jnp.bfloat16).astype(jnp.float32)
    return high, middle, rest - middle


def fill_constants(spread, sums):
    sub = lax.broadcasted_iota(jnp.int32, (64, TILE), 0)
    for c in range(FIELDS):
        here = (lax.rem(sub, 16) == c) & (sub < 48)
        for ref in spread:
            ref[:, c * TILE : (c + 1) * TILE] = here.astype(jnp.float32).astype(jnp.bfloat16)
    row = lax.broadcasted_iota(jnp.int32, (16, 6 * TILE), 0)
    column = lax.rem(lax.broadcasted_iota(jnp.int32, (16, 6 * TILE), 1) // (TILE // 2), 6)
    sums[...] = (row == column).astype(jnp.float32).astype(jnp.bfloat16)


def combine(rec_i, rec_j, spread, both):
    high, middle, low = split(rec_i)
    sub = lax.broadcasted_iota(jnp.int32, (16, TILE), 0)
    for c in range(10):
        rows = jnp.where(
            sub == 0,
            high[c : c + 1],
            jnp.where(sub == 1, middle[c : c + 1], jnp.where(sub == 2, low[c : c + 1], 0.0)),
        )
        if c < 6:
            rows = -rows
        spread[48:64, c * TILE : (c + 1) * TILE] = rows.astype(jnp.bfloat16)
    high, middle, low = split(rec_j)
    left = jnp.concatenate(
        [high, middle, low, jnp.ones((16, TILE), jnp.float32), jnp.zeros((64, TILE), jnp.float32)], axis=0
    )
    left = jnp.transpose(left)[:, 0:64].astype(jnp.bfloat16)
    both[...] = jnp.dot(left, spread[...], preferred_element_type=jnp.float32)


def fold(first, second):
    low = lax.broadcasted_iota(jnp.int32, first.shape, 1) < TILE // 2
    kept = jnp.where(low, first, second)
    other = jnp.where(low, second, first)
    return kept + pltpu.roll(other, TILE // 2, 1)


def pair_forces(rec_i, words, both, parts):
    radius_i = rec_i[9:10, :]
    scaled = damping_tangent * damping_tangent * radius_i
    sub = lax.broadcasted_iota(jnp.int32, (8, TILE), 0)
    bit = jnp.left_shift(1, sub)
    sums_i = [jnp.zeros((8, TILE), jnp.float32) for _ in range(6)]
    for first in range(0, TILE, BLOCK):
        field = [both[first : first + BLOCK, c * TILE : (c + 1) * TILE] for c in range(FIELDS)]
        r, dv, spin = field[0:3], field[3:6], field[6:9]
        d2 = r[0] * r[0] + r[1] * r[1] + (r[2] * r[2] + softening * softening)
        inv = lax.rsqrt(d2)
        inter = jnp.maximum(field[9] - d2 * inv, 0.0)
        top = (field[9] - radius_i) * scaled * inter
        root = top * lax.rsqrt(jnp.maximum(top * field[9], 1e-30))
        hit = jnp.concatenate(
            [
                (jnp.broadcast_to(words[w : w + 1, :], (8, TILE)) & bit) != 0
                for w in range(first // 8, (first + BLOCK) // 8)
            ],
            axis=0,
        )
        k2 = jnp.where(hit, root, 0.0)
        n = [inv * x for x in r]
        speed_n = dv[0] * n[0] + dv[1] * n[1] + dv[2] * n[2]
        k1 = k2 * (
            (stiffness / damping_tangent) * inter
            - ((damping_normal - damping_tangent) / damping_tangent) * speed_n
        )
        turn = cross(spin, n)
        drag = [k2 * (dv[c] - turn[c]) for c in range(3)]
        terms = [drag[c] - k1 * n[c] for c in range(3)] + list(cross(n, drag))
        for c in range(6):
            part = terms[c]
            sums_i[c] = sums_i[c] + sum(part[8 * q : 8 * q + 8] for q in range(BLOCK // 8))
        for c in range(3):
            part = fold(terms[2 * c], terms[2 * c + 1])
            high = part.astype(jnp.bfloat16)
            low = (part - high.astype(jnp.float32)).astype(jnp.bfloat16)
            parts[first : first + BLOCK, c * TILE : (c + 1) * TILE] = high
            parts[first : first + BLOCK, (3 + c) * TILE : (4 + c) * TILE] = low
    own = jnp.zeros((8, TILE), jnp.float32)
    for c in range(6):
        own = jnp.where(sub == c, jnp.sum(sums_i[c], axis=0, keepdims=True), own)
    own = own * jnp.where(sub < 3, 1.0, radius_i)
    return own


def forces_back(rec_j, parts, sums):
    over = (((1,), (1,)), ((), ()))
    back = lax.dot_general(sums[...], parts[...], over, preferred_element_type=jnp.float32)
    sub = lax.broadcasted_iota(jnp.int32, (8, TILE), 0)
    return back[0:8] * jnp.where(sub < 3, -1.0, rec_j[9:10, :])


def load_tiles(table, first, number, record, moved=None, shifts=()):
    def rows(ref, c):
        return ref[c * number : (c + 1) * number, :]

    radius = rows(record, 9)
    live = jnp.where(radius > 0.0, 1.0, 0.0)
    for c in range(10):
        if c == 9:
            value = radius
        elif moved is None:
            value = rows(record, c)
        elif c < 3:
            value = rows(record, c) + time_step * live * rows(moved, c)
        else:
            value = rows(moved, c - 3)
        if 6 <= c < 9:
            value = value * radius
        if c < 2 and shifts:
            value = jnp.concatenate([value[32 * k : 32 * k + 32] + at[c] for k, at in enumerate(shifts)], axis=0)
        table[pl.ds(first * 16 + c, number, stride=16), :] = value


def run_pairs(table, force, masks, chosen, partners, skipped, scratch, part):
    spread, both, parts = (scratch[k * UNROLL : (k + 1) * UNROLL] for k in range(3))
    sums = scratch[3 * UNROLL]
    fill_constants(spread, sums)
    last = force.shape[0] // 8 - 1
    table[last * 16 : last * 16 + 16] = jnp.full((16, TILE), DEAD, jnp.float32)
    force[last * 8 : last * 8 + 8] = jnp.zeros((8, TILE), jnp.float32)

    found = chosen[128]
    origin, number = found * part[0] // part[2], found * part[1] // part[2]

    def entry(n):
        real = n + origin < number
        p = jnp.where(real, chosen[jnp.minimum(n + origin, 127)], 0)
        owner = jnp.where(real, p // 2, last)
        place = jnp.where(real, partners[p] - skipped, last)
        return p, owner, place

    def record(tile):
        return table[pl.ds(pl.multiple_of(tile * 16, 16), 16), :]

    def prepare(item, spread, both):
        combine(record(item[1]), record(item[2]), spread, both)

    def forces(item, both, parts):
        return pair_forces(record(item[1]), masks[item[0]], both, parts)

    def back(place, parts):
        return forces_back(record(place), parts, sums)

    def add(tile, value):
        at = pl.ds(pl.multiple_of(tile * 8, 8), 8)
        force[at, :] = force[at, :] + value

    parts[-1][...] = jnp.zeros_like(parts[-1])
    prepare(entry(0), spread[0], both[0])

    def some(t, before):
        items = [entry(UNROLL * t + k) for k in range(UNROLL + 1)]
        results = []
        place = before
        for k in range(UNROLL):
            after = (k + 1) % UNROLL
            prepare(items[k + 1], spread[after], both[after])
            results.append((place, back(place, parts[k - 1])))
            results.append((items[k][1], forces(items[k], both[k], parts[k])))
            place = items[k][2]
        for tile, value in results:
            add(tile, value)
        return place

    final = lax.fori_loop(0, (number - origin + UNROLL - 1) // UNROLL, some, jnp.int32(last))
    add(final, back(final, parts[-1]))


def pair_scratch(tiles):
    return [
        pltpu.VMEM(((tiles + 1) * 16, TILE), jnp.float32),
        pltpu.VMEM(((tiles + 1) * 8, TILE), jnp.float32),
        *[pltpu.VMEM((64, FIELDS * TILE), jnp.bfloat16)] * UNROLL,
        *[pltpu.VMEM((TILE, FIELDS * TILE), jnp.float32)] * UNROLL,
        *[pltpu.VMEM((TILE, 6 * TILE), jnp.bfloat16)] * UNROLL,
        pltpu.VMEM((16, 6 * TILE), jnp.bfloat16),
    ]


def scan(low, high, partners, alive, chosen):
    def some(block, found):
        pairs = [block * 16 + k for k in range(16)]
        slots = [partners[p] for p in pairs]
        owners = [alive[block * 8 + k] for k in range(8)]
        others = [alive[slot] for slot in slots]
        for k in range(16):
            good = (slots[k] >= low) & (slots[k] < high) & (owners[k // 2] + others[k] == 2)
            chosen[found] = pairs[k]
            found = found + good.astype(jnp.int32)
        return found

    chosen[128] = lax.fori_loop(0, 8, some, 0)


def by_field(target, force, number):
    for c in range(6):
        target[c * number : (c + 1) * number, :] = force[pl.ds(c, number, stride=8), :]


def by_tile(target, at, force, first, number):
    for k in range(number):
        target[(at + k) * 6 : (at + k) * 6 + 6, :] = force[(first + k) * 8 : (first + k) * 8 + 6, :]


def pairs_kernel(kind, part, listed, pushed, *refs):
    refs = list(refs)
    partners, chosen, shift, masks, start = (refs.pop(0) for _ in range(5))
    sides = [refs.pop(0) for _ in range(2)] if kind == "far" else ()
    ghosts = {"own": 0, "x": 1, "y": 2, "far": 2}[kind]
    records = [refs.pop(0) for _ in range(1 + ghosts)]
    moved = [refs.pop(0) for _ in range(1 + ghosts)] if pushed else [None] * (1 + ghosts)
    number = 0 if kind == "own" else 32 if kind == "y" else 64
    low = {"own": 0, "x": 64, "y": 128, "far": 192}[kind]
    own_force = refs.pop(0)
    outs = [refs.pop(0) for _ in range(ghosts)]
    if not listed:
        alive, chosen = chosen, refs.pop(0)
        scan(low, low + ghosts * number if ghosts else 64, partners, alive, chosen)
    table, force, *scratch = refs
    tiles = 64 + ghosts * number
    table[...] = jnp.zeros_like(table)
    load_tiles(table, 0, 64, records[0], moved[0])
    for k in range(ghosts):
        if kind == "x":
            shifts = ((shift[0], 0.0), (shift[1], 0.0))
        elif kind == "y":
            shifts = ((0.0, shift[2 + k]),)
        else:
            shifts = ((shift[0], shift[2 + k]), (shift[1], shift[2 + k]))
        load_tiles(table, 64 + k * number, number, records[1 + k], moved[1 + k], shifts)
    force[0:512] = start[...]
    if ghosts:
        force[512 : tiles * 8] = jnp.zeros((tiles * 8 - 512, TILE), jnp.float32)
    run_pairs(table, force, masks, chosen, partners, max(low - 64, 0), scratch, part)
    if own_force.shape[0] == 384:
        by_field(own_force, force, 64)
    else:
        own_force[...] = force[0:512]
    for k in range(ghosts):
        if kind == "x":
            outs[k][...] = force[512:1024]
        elif kind == "y":
            by_tile(outs[k], 0, force, 64 + 32 * k, 32)
            clear_spare(outs[k])
        else:
            outs[k][0:192] = sides[k][0:192]
            by_tile(outs[k], 32, force, 64 + 64 * k, 64)
            clear_spare(outs[k])


def shape(*dims):
    return jax.ShapeDtypeStruct(dims, jnp.float32)


def pairs(kind, partners, listing, shift, masks, start, records, moved=(), sides=(), part=(0, 1, 1), last=False):
    listed = listing.shape[0] == 136
    outs = {"own": [], "x": [512], "y": [192 + SPARE] * 2, "far": [576 + SPARE] * 2}[kind]
    shapes = [shape(rows, TILE) for rows in [384 if last else 512] + outs]
    places = [VMEM] * len(shapes)
    if not listed:
        shapes.append(jax.ShapeDtypeStruct((136,), jnp.int32))
        places.append(SMEM)
    return pl.pallas_call(
        functools.partial(pairs_kernel, kind, part, listed, bool(moved)),
        out_shape=shapes,
        in_specs=[SMEM] * 3 + [VMEM] * (2 + len(sides) + len(records) + len(moved)),
        out_specs=places,
        scratch_shapes=pair_scratch({"own": 64, "x": 128, "y": 128, "far": 192}[kind]),
        compiler_params=params(),
        cost_estimate=cost(60_000_000, 2_000_000),
        name=kind + "_pairs",
    )(partners, listing, shift, masks, start, *sides, *records, *moved)


def pack_kernel(count, position, velocity, spin, radius, exports, packed, lists, sems):
    moves = [(position, 0, 192), (velocity, 192, 192), (spin, 384, 192), (radius, 576, 64)]
    copies = [
        pltpu.make_async_copy(source, packed.at[pl.ds(first, rows)], sems.at[k])
        for k, (source, first, rows) in enumerate(moves)
    ]
    copies.append(pltpu.make_async_copy(exports, lists, sems.at[4]))
    for copy in copies:
        copy.start()
    packed[640:648] = jnp.zeros((8, TILE), jnp.float32)
    at = (64, TILE)
    index = lax.broadcasted_iota(jnp.int32, at, 0) * TILE + lax.broadcasted_iota(jnp.int32, at, 1)
    for copy in copies:
        copy.wait()
    packed[576:640] = jnp.where(index < count[0, 0], packed[576:640], DEAD)
    packed[640:648, 0:32] = lists[...].astype(jnp.float32)


def pack(count, position, velocity, spin, radius, exports):
    return pl.pallas_call(
        pack_kernel,
        out_shape=shape(648, TILE),
        in_specs=[SMEM] + [pl.BlockSpec(memory_space=pltpu.HBM)] * 5,
        out_specs=VMEM,
        scratch_shapes=[pltpu.VMEM((8, 32), jnp.int32), pltpu.SemaphoreType.DMA((5,))],
        compiler_params=pltpu.CompilerParams(vmem_limit_bytes=65_800_000),
        cost_estimate=cost(100_000, 700_000),
        name="pack",
    )(count, position, velocity, spin, radius, exports)


SPARE = 8


def clear_spare(*refs):
    for ref in refs:
        ref[ref.shape[0] - SPARE : ref.shape[0], :] = jnp.zeros((SPARE, TILE), jnp.float32)


def copy_tile(rows, source, tile, target, place, width):
    for c in range(rows):
        target[pl.ds(c * width + place, 1), :] = source[pl.ds(c * 64 + tile, 1), :]


def pick_own_kernel(rows, lists, own, even, odd):
    clear_spare(even, odd)

    def some(block, carry):
        for k in range(4):
            e = block * 4 + k
            copy_tile(rows, own, lists[e], even, e, 32)
            copy_tile(rows, own, lists[96 + e], odd, e, 32)
        return carry

    lax.fori_loop(0, 8, some, 0)


def pick_kernel(rows, lists, near, next_, even, odd, ghost):
    sources = (near, next_)
    clear_spare(even, odd, ghost)

    def some(block, carry):
        for k in range(4):
            e = block * 4 + k
            for which in range(2):
                place = which * 32 + e
                copy_tile(rows, sources[which], lists[32 + place], even, place, 64)
                copy_tile(rows, sources[which], lists[128 + place], odd, place, 64)
                copy_tile(rows, sources[which], lists[192 + place], ghost, place, 64)
        return carry

    lax.fori_loop(0, 8, some, 0)


def pick_own(rows, lists, own):
    return pl.pallas_call(
        functools.partial(pick_own_kernel, rows),
        out_shape=(shape(rows * 32 + SPARE, TILE),) * 2,
        in_specs=[SMEM, VMEM],
        out_specs=(VMEM,) * 2,
        compiler_params=params(),
        cost_estimate=cost(1_000_000, 1_000_000),
        name="pick_own",
    )(lists, own)


def pick(rows, lists, near, next_):
    return pl.pallas_call(
        functools.partial(pick_kernel, rows),
        out_shape=(shape(rows * 64 + SPARE, TILE),) * 3,
        in_specs=[SMEM, VMEM, VMEM],
        out_specs=(VMEM,) * 3,
        compiler_params=params(),
        cost_estimate=cost(1_000_000, 3_000_000),
        name="pick",
    )(lists, near, next_)


def gather_kernel(lists, ghost, even, odd, own_total, near, next_, *sums):
    for ref in sums:
        ref[...] = jnp.zeros_like(ref)

    def add(ref, tile, value):
        at = pl.ds(pl.multiple_of(tile * 8, 8), value.shape[0])
        ref[at, :] = ref[at, :] + value

    def some(block, carry):
        for k in range(4):
            e = block * 4 + k
            for which in range(3):
                place = which * 32 + e
                add(sums[which], lists[place], even[pl.ds(place * 6, 6), :])
                add(sums[3 + which], lists[96 + place], odd[pl.ds(place * 6, 6), :])
            for which in range(2):
                place = which * 32 + e
                value = ghost[pl.ds(pl.multiple_of(place * 8, 8), 8), :]
                add(sums[6 + which], lists[192 + place], value)
        return carry

    lax.fori_loop(0, 8, some, 0)
    for c in range(6):
        part = [ref[pl.ds(c, 64, stride=8), :] for ref in sums]
        own_total[c * 64 : (c + 1) * 64, :] = part[0] + part[3]
        near[c * 64 : (c + 1) * 64, :] = part[1] + part[4] + part[6]
        next_[c * 64 : (c + 1) * 64, :] = part[2] + part[5] + part[7]


def gather(lists, ghost, even, odd):
    return pl.pallas_call(
        gather_kernel,
        out_shape=(shape(384, TILE),) * 3,
        in_specs=[SMEM, VMEM, VMEM, VMEM],
        out_specs=(VMEM,) * 3,
        scratch_shapes=[pltpu.VMEM((512, TILE), jnp.float32)] * 8,
        compiler_params=params(),
        cost_estimate=cost(1_000_000, 3_000_000),
        name="gather",
    )(lists, ghost, even, odd)


def local(positions, velocities, spins, radii, counts, exports, partners, masks):
    tiles = radii.shape[-1] // TILE
    count = counts[0, 0]
    chosen = exports[0, 0]
    words = masks[0, 0]
    packed = pack(
        counts,
        positions.reshape(3 * tiles, TILE),
        velocities.reshape(3 * tiles, TILE),
        spins.reshape(3 * tiles, TILE),
        radii.reshape(tiles, TILE),
        chosen,
    )
    got_y = swap(packed, "gx", 1)
    got_x = swap(packed, "gx", 0)
    state = packed
    position, velocity, spin = (packed[k * tiles : (k + 3) * tiles].reshape(3, tiles, TILE) for k in (0, 3, 6))
    radius = packed[9 * tiles : 10 * tiles].reshape(1, tiles, TILE)
    live = (radius > 0.0).astype(jnp.float32)
    mass = mass_scale * radius * radius * radius
    inertia = 0.4 * mass * radius * radius
    lift = jnp.array([0.0, 0.0, -gravity], jnp.float32)[:, None, None]

    odd_x = lax.rem(lax.axis_index("gx"), 2)
    odd_y = lax.rem(lax.axis_index("gy"), 2)
    east = {0: odd_x == 1, 1: odd_x == 0}
    north = {0: odd_y == 0, 1: odd_y == 1}

    def choose(table, which):
        return lax.dynamic_index_in_dim(table, which, 0, keepdims=False)

    def face(a):
        return jnp.where(a, 0, 1)

    def side(b):
        return jnp.where(b, 2, 3)

    def corner(a, b):
        return jnp.where(a, jnp.where(b, 4, 5), jnp.where(b, 6, 7))

    west_at = jnp.where(odd_x == 1, 0, 1)
    south_at = jnp.where(odd_y == 1, 0, 1)
    x_of = (west_at, 1 - west_at)
    y_of = (south_at, 1 - south_at)
    block_of = [
        x_of[0],
        x_of[1],
        2 + y_of[0],
        2 + y_of[1],
        4 + 2 * y_of[0] + x_of[0],
        4 + 2 * y_of[1] + x_of[0],
        4 + 2 * y_of[0] + x_of[1],
        4 + 2 * y_of[1] + x_of[1],
    ]
    block_of = jnp.stack(block_of).astype(jnp.int32)
    listed = partners[0, 0]
    kind = jnp.maximum(listed - tiles, 0) // 32
    hot = (kind[:, None] == jnp.arange(8, dtype=jnp.int32)[None, :]).astype(jnp.int32)
    slots = jnp.where(
        listed < tiles,
        listed,
        tiles + 32 * jnp.sum(hot * block_of[None, :], axis=1) + lax.rem(jnp.maximum(listed - tiles, 0), 32),
    )
    own_alive = (jnp.arange(tiles, dtype=jnp.int32) * TILE < count).astype(jnp.int32)

    shift = jnp.stack(
        [
            jnp.where(east[0], -column_width, column_width),
            jnp.where(east[1], -column_width, column_width),
            jnp.where(north[0], column_width, -column_width),
            jnp.where(north[1], column_width, -column_width),
        ]
    ).astype(jnp.float32)
    nothing = jnp.zeros((tiles * 8, TILE), jnp.float32)

    def alive_in(record):
        number = record.shape[0] // 10
        return (record[9 * number : 10 * number, 0] > 0.0).astype(jnp.int32)

    def exchange_sides(rows, lists, own):
        to_even, to_odd = pick_own(rows, lists, own)
        return swap(to_even, "gy", 0), swap(to_odd, "gy", 1)

    own_lists = [choose(chosen, side(north[0])), choose(chosen, side(north[1]))]

    for step in range(STEPS):
        if step == 0:
            blank = jnp.zeros((64,), jnp.int32)
            lists = jnp.concatenate([own_lists[0], blank, own_lists[1], blank, blank])
            even_side, odd_side = exchange_sides(10, lists, state)
            list_x = got_x[10 * tiles :, 0:32].astype(jnp.int32)
            list_y = got_y[10 * tiles :, 0:32].astype(jnp.int32)
            lists = jnp.stack(
                [
                    own_lists[0],
                    choose(list_x, corner(east[0], north[0])),
                    choose(list_y, corner(east[1], north[0])),
                    own_lists[1],
                    choose(list_x, corner(east[0], north[1])),
                    choose(list_y, corner(east[1], north[1])),
                    choose(list_x, face(east[0])),
                    choose(list_y, face(east[1])),
                ]
            ).reshape(256)
            to_even, to_odd, ghost = pick(10, lists, got_x, got_y)
            even, odd = swap(to_even, "gy", 0), swap(to_odd, "gy", 1)
            alive = jnp.concatenate([own_alive, alive_in(ghost), alive_in(even_side), alive_in(odd_side)])
            near_alive = jnp.concatenate([alive, jnp.zeros((128,), jnp.int32)])
            own_force, *sides, y_list = pairs(
                "y", slots, near_alive, shift, words, nothing, (state, even_side, odd_side)
            )
            even, odd, own_force = lax.optimization_barrier((even, odd, own_force))
            far_alive = jnp.concatenate([alive, alive_in(even), alive_in(odd)])
            own_force, even_force, odd_force, far_list = pairs(
                "far", slots, far_alive, shift, words, own_force, (state, even, odd), (), sides
            )
            back_odd, back_even = swap(odd_force, "gy", 1), swap(even_force, "gy", 0)
            own_force, ghost_force, x_list = pairs("x", slots, near_alive, shift, words, own_force, (state, ghost))
        else:
            new = jnp.concatenate([velocity, spin], axis=0).reshape(6 * tiles, TILE)
            new = jnp.concatenate([new, jnp.zeros((SPARE, TILE), jnp.float32)])
            got_y = swap(new, "gx", 1)
            got_x = swap(new, "gx", 0)
            to_even, to_odd = pick_own(6, lists, new)
            even_side_new, odd_side_new = swap(to_even, "gy", 0), swap(to_odd, "gy", 1)
            early, _ = lax.optimization_barrier((nothing, to_even))
            own_force = pairs(
                "own", slots, own_list, shift, words, early, (state,), (new,), part=SECOND_PARTS[0]
            )[0]
            got_x, got_y, even_side_new, odd_side_new, own_force = lax.optimization_barrier(
                (got_x, got_y, even_side_new, odd_side_new, own_force)
            )
            to_even, to_odd, ghost_new = pick(6, lists, got_x, got_y)
            even_new, odd_new = swap(to_even, "gy", 0), swap(to_odd, "gy", 1)
            own_force, _ = lax.optimization_barrier((own_force, to_even))
            own_force, *sides = pairs(
                "y",
                slots,
                y_list,
                shift,
                words,
                own_force,
                (state, even_side, odd_side),
                (new, even_side_new, odd_side_new),
            )
            even_new, odd_new, own_force = lax.optimization_barrier((even_new, odd_new, own_force))
            own_force, even_force, odd_force = pairs(
                "far", slots, far_list, shift, words, own_force, (state, even, odd), (new, even_new, odd_new), sides
            )
            back_odd, back_even = swap(odd_force, "gy", 1), swap(even_force, "gy", 0)
            own_force, ghost_force = pairs(
                "x", slots, x_list, shift, words, own_force, (state, ghost), (new, ghost_new)
            )
        back_odd, back_even, own_force = lax.optimization_barrier((back_odd, back_even, own_force))
        own_total, to_x, to_y = gather(lists, ghost_force, back_even, back_odd)
        back_y = swap(to_y, "gx", 1)
        back_x = swap(to_x, "gx", 0)
        own_total, own_force = lax.optimization_barrier((own_total, own_force))
        if step == 0:
            last_force, own_list = pairs("own", slots, near_alive, shift, words, own_force, (state,), last=True)
        else:
            (last_force,) = pairs(
                "own",
                slots,
                own_list,
                shift,
                words,
                own_force,
                (state,),
                (new,),
                part=SECOND_PARTS[1],
                last=True,
            )
        force = sum(part.reshape(6, tiles, TILE) for part in (own_total, back_x, back_y, last_force))
        velocity = velocity + time_step * live * (force[0:3] / mass + lift)
        spin = spin + time_step * live * force[3:6] / inertia
        position = position + time_step * live * velocity
    result = (1, 1, 3, tiles * TILE)
    return (position.reshape(result), velocity.reshape(result), spin.reshape(result))


def solution(mesh):
    return jax.shard_map(
        local,
        mesh=mesh,
        in_specs=(
            P("gx", "gy", None, None),
            P("gx", "gy", None, None),
            P("gx", "gy", None, None),
            P("gx", "gy", None),
            P("gx", "gy"),
            P("gx", "gy", None, None),
            P("gx", "gy", None),
            P("gx", "gy", None, None, None),
        ),
        out_specs=(P("gx", "gy", None, None), P("gx", "gy", None, None), P("gx", "gy", None, None)),
        check_vma=False,
    )
```
